256 devices in a mesh: ctx: 32 (over x, z), uly: 8 (over y, core).
Axes of the slice: x: 4, y: 4, z: 8, core: 2. Of those that a mesh axis runs over, the one named last changes fastest.
Arguments:
- queries: bfloat16 [32768, 7168], P(('ctx', 'uly')), may hold values from -6 to 6
- keys: bfloat16 [32768, 1024], P(('ctx', 'uly')), may hold values from -6 to 6
- values: bfloat16 [32768, 1024], P(('ctx', 'uly')), may hold values from -30 to 30
- cotangent: bfloat16 [32768, 7168], P(('ctx', 'uly')), may hold values from -6 to 6
- norm_gain: float32 [7168], replicated, may hold values from 0.1 to 1.9
- owner_of_row: int32 [32768], P('ctx'), may hold values from 0 to 31, as said below
- arrival: int32 [32768], P('ctx'), may hold values from 0 to 2047, as said below
- doc_start: int32 [32768], P('ctx'), may hold values from 0 to 1023, as said below
Outputs:
- normed: bfloat16 [32768, 7168], P(('ctx', 'uly'))
- grad_queries: bfloat16 [32768, 7168], P(('ctx', 'uly'))
- grad_keys: bfloat16 [32768, 1024], P(('ctx', 'uly'))
- grad_values: bfloat16 [32768, 1024], P(('ctx', 'uly'))
- grad_gain: float32 [7168], replicated
The draws below stay inside these ranges and needn't reach their ends.
Inputs may be any that keep to these rules, and one draw needn't show every extreme that they name: `owner_of_row`: each owner gets exactly 1024 rows in all and at most 64 rows of one group; some group sends exactly 64 rows to each owner. `arrival`: consistent with owner_of_row as the steps state; the values of one owner are distinct. `doc_start`: documents are runs of 1 to 512 slots within one owner; every owner holds one document of exactly 512 slots.
All inputs are finite; a program needn't handle non-finite values.
Results may differ from the reference program's by a relative error of at most 0.012.
Values may be sent and summed in bfloat16 or wider, within the bound.
No kernel may reach another device: no remote copies, remote signals or barrier semaphores. Data moves between devices by JAX's collectives and lax.ppermute only.
A program may use at most 192 MiB of HBM per device.

```python
import jax
import jax.numpy as jnp
from jax import lax

QUERY_HEADS = 56
KEY_VALUE_HEADS = 8
HEAD_DIMENSION = 128
TOK_DEV = 128
WIDTH = 7168
ROWS_PER_GROUP = 1024
CAP = 64
DOC_MAX = 512
TOTAL_TOKENS = 32768
N_CTX = 32
N_ULY = 8


def plan_tables(key):
    key = jax.random.fold_in(key, 11)
    group_rows = TOK_DEV * N_ULY
    base_count = group_rows // N_CTX
    random_key_array = jax.random.split(key, 4)
    owner_ids = jnp.arange(N_CTX, dtype=jnp.int32)
    order_perm = jax.random.permutation(random_key_array[0], N_CTX).astype(jnp.int32)
    following = jnp.roll(order_perm, -1)
    counts = base_count + base_count * (owner_ids[None, :] == order_perm[:, None]).astype(jnp.int32) - base_count * (owner_ids[None, :] == following[:, None]).astype(jnp.int32)
    cum_counts = jnp.cumsum(counts, axis=1)
    slot_ids = jnp.arange(group_rows, dtype=jnp.int32)
    listed = jnp.sum((slot_ids[None, None, :] >= cum_counts[:, :, None]).astype(jnp.int32), axis=1)

    def shuffle_row(sub_key, row_values):
        return jax.random.permutation(sub_key, row_values)
    owners = jax.vmap(shuffle_row)(jax.random.split(random_key_array[1], N_CTX), listed).astype(jnp.int32)
    onehot = (owners[:, :, None] == owner_ids[None, None, :]).astype(jnp.int32)
    row_rank = jnp.sum((jnp.cumsum(onehot, axis=1) - onehot) * onehot, axis=2)
    arrive = owner_ids[:, None] * CAP + row_rank
    before = jnp.cumsum(counts, axis=0) - counts
    incoming = jnp.take_along_axis(before, owners, axis=1) + row_rank

    def slot_order(sub_key):
        return jax.random.permutation(sub_key, group_rows).astype(jnp.int32)
    slot_perm = jax.vmap(slot_order)(jax.random.split(random_key_array[2], N_CTX))
    slots = slot_perm[owners, incoming]
    arrival = jnp.zeros((N_CTX, group_rows), jnp.int32).at[owners, slots].set(arrive)
    min_length = max(1, DOC_MAX // 16)
    piece_count = group_rows // min_length + 2

    def doc_first(sub_key):
        key_a, key_b = jax.random.split(sub_key)
        lengths = jax.random.randint(key_a, (piece_count,), min_length, DOC_MAX + 1)
        long_index = jax.random.randint(key_b, (), 0, 2)
        lengths = jnp.where(jnp.arange(piece_count) == long_index, DOC_MAX, lengths).astype(jnp.int32)
        begins = jnp.cumsum(lengths) - lengths
        doc_marks = jnp.zeros((group_rows,), jnp.int32).at[begins].set(1, mode='drop')
        return lax.cummax(jnp.where(doc_marks > 0, slot_ids, 0), axis=0)
    doc_table = jax.vmap(doc_first)(jax.random.split(random_key_array[3], N_CTX))
    return (owners.reshape(-1), arrival.reshape(-1), doc_table.reshape(-1))


def draw_owner_of_row(key, part):
    return plan_tables(key)[0]


def draw_arrival(key, part):
    return plan_tables(key)[1]


def draw_doc_start(key, part):
    return plan_tables(key)[2]


def draw_queries(key, part):
    key = jax.random.fold_in(key, 1)
    initial_sample = jax.random.normal(key, (TOTAL_TOKENS, QUERY_HEADS * HEAD_DIMENSION), jnp.float32)
    return jnp.clip(initial_sample, -4.0, 4.0).astype(jnp.bfloat16)


def draw_keys(key, part):
    key = jax.random.fold_in(key, 2)
    initial_sample = jax.random.normal(key, (TOTAL_TOKENS, KEY_VALUE_HEADS * HEAD_DIMENSION), jnp.float32)
    return jnp.clip(initial_sample, -4.0, 4.0).astype(jnp.bfloat16)


def draw_values(key, part):
    key = jax.random.fold_in(key, 3)
    random_key_array = jax.random.split(key, 3)
    row_scale = jnp.exp(jax.random.uniform(random_key_array[0], (TOTAL_TOKENS, 1), jnp.float32, 0.0, 2.302585))
    column_scale = jnp.exp(jax.random.uniform(random_key_array[1], (1, KEY_VALUE_HEADS * HEAD_DIMENSION), jnp.float32, 0.0, 2.302585))
    initial_sample = jnp.clip(jax.random.normal(random_key_array[2], (TOTAL_TOKENS, KEY_VALUE_HEADS * HEAD_DIMENSION), jnp.float32), -3.0, 3.0)
    return (initial_sample * row_scale * column_scale / 10.0).astype(jnp.bfloat16)


def level_of(key, dims, cuts, least, largest):
    def one(dim, parts):
        draws = jax.random.uniform(jax.random.fold_in(jax.random.fold_in(key, 6), dim), (parts,), jnp.float32, least / len(cuts), largest / len(cuts))
        return jnp.repeat(jnp.exp(draws), dims[dim] // parts).reshape((-1,) + (1,) * (len(dims) - dim - 1))

    factor_of = one(*cuts[0])
    for cut in cuts[1:]:
        factor_of = factor_of * one(*cut)
    return factor_of


def noise(rng, shape, width, most, cuts=(), kind=jnp.bfloat16):
    drawn = width * jax.random.normal(rng, shape, jnp.float32)
    if cuts:
        drawn = drawn * level_of(rng, shape, cuts, -0.22, 0.18)
    return jnp.clip(drawn, -most, most).astype(kind)


def setup_inputs(seed: int = 0) -> dict:
    seeds = jax.random.split(jax.random.key(seed), 9)
    return {
        "queries": draw_queries(jax.random.fold_in(seeds[8], 71), 0),
        "keys": draw_keys(jax.random.fold_in(seeds[8], 71), 0),
        "values": draw_values(jax.random.fold_in(seeds[8], 71), 0),
        "cotangent": noise(seeds[3], (TOTAL_TOKENS, WIDTH), 1.0, 6.0, ((0, 256),)),
        "norm_gain": jnp.clip(1.0 + 0.18 * jax.random.normal(seeds[4], (WIDTH,), jnp.float32), 0.1, 1.9),
        "owner_of_row": draw_owner_of_row(jax.random.fold_in(seeds[8], 71), 0),
        "arrival": draw_arrival(jax.random.fold_in(seeds[8], 71), 0),
        "doc_start": draw_doc_start(jax.random.fold_in(seeds[8], 71), 0),
    }


def block_weights(query_blk, key_win, first_key, query_pos, key_pos, score_scale):
    scores = jnp.einsum('qngd,knd->ngqk', query_blk, key_win) * score_scale
    allowed = (key_pos[None, :] >= first_key[:, None]) & (key_pos[None, :] <= query_pos[:, None])
    scores = jnp.where(allowed, scores, -jnp.inf)
    row_peak = lax.optimization_barrier(jnp.max(scores, axis=-1, keepdims=True))
    log_total = row_peak + jnp.log(lax.optimization_barrier(jnp.sum(jnp.exp(scores - row_peak), axis=-1, keepdims=True)))
    return jnp.exp(scores - log_total)

def owner_pass(query_row_block, key_row_block, value_row_block, cot_rows, doc_first, norm_gain):
    group_extent = QUERY_HEADS // KEY_VALUE_HEADS
    block_len = DOC_MAX
    window = 2 * DOC_MAX
    score_scale = HEAD_DIMENSION ** (-0.5)
    query_head = query_row_block.reshape(ROWS_PER_GROUP, KEY_VALUE_HEADS, group_extent, HEAD_DIMENSION).astype(jnp.float32)
    key_head = key_row_block.reshape(ROWS_PER_GROUP, KEY_VALUE_HEADS, HEAD_DIMENSION).astype(jnp.float32)
    value_head = value_row_block.reshape(ROWS_PER_GROUP, KEY_VALUE_HEADS, HEAD_DIMENSION).astype(jnp.float32)
    starts = jnp.arange(ROWS_PER_GROUP // block_len, dtype=jnp.int32) * block_len

    def pieces(row_start):
        win_start = jnp.clip(row_start - block_len, 0, ROWS_PER_GROUP - window).astype(jnp.int32)
        query_blk = lax.dynamic_slice_in_dim(query_head, row_start, block_len, 0)
        key_win = lax.dynamic_slice_in_dim(key_head, win_start, window, 0)
        value_win = lax.dynamic_slice_in_dim(value_head, win_start, window, 0)
        first_key = lax.dynamic_slice_in_dim(doc_first, row_start, block_len, 0)
        query_pos = row_start + jnp.arange(block_len, dtype=jnp.int32)
        key_pos = win_start + jnp.arange(window, dtype=jnp.int32)
        weights = block_weights(query_blk, key_win, first_key, query_pos, key_pos, score_scale)
        rounded = lax.optimization_barrier(weights.astype(jnp.bfloat16)).astype(jnp.float32)
        return (win_start, query_blk, key_win, value_win, weights, rounded)

    def forward(row_start):
        win_start, query_blk, key_win, value_win, weights, rounded = pieces(row_start)
        result = jnp.einsum('ngqk,knd->qngd', rounded, value_win)
        return result.astype(jnp.bfloat16).reshape(block_len, QUERY_HEADS * HEAD_DIMENSION)
    attended = lax.map(forward, starts).reshape(ROWS_PER_GROUP, QUERY_HEADS * HEAD_DIMENSION)
    attended_wide = lax.optimization_barrier(attended).astype(jnp.float32)
    norm_root = jnp.sqrt(lax.optimization_barrier(jnp.sum(attended_wide * attended_wide, axis=1)) / WIDTH + 1e-06)[:, None]
    normed_rows = (norm_gain * attended_wide / norm_root).astype(jnp.bfloat16)
    cot_wide = cot_rows.astype(jnp.float32)
    cross_term = lax.optimization_barrier(jnp.sum(norm_gain * cot_wide * attended_wide, axis=1))[:, None]
    attention_gradient = norm_gain * cot_wide / norm_root - attended_wide * (cross_term / (WIDTH * norm_root ** 3))
    attention_gradient = lax.optimization_barrier(attention_gradient.astype(jnp.bfloat16))
    gain_part = lax.optimization_barrier(jnp.sum(cot_wide * attended_wide / norm_root, axis=0))
    cotangent_head = attention_gradient.astype(jnp.float32).reshape(ROWS_PER_GROUP, KEY_VALUE_HEADS, group_extent, HEAD_DIMENSION)

    def backward(carry, row_start):
        key_gradient, value_gradient = carry
        win_start, query_blk, key_win, value_win, weights, rounded = pieces(row_start)
        cot_blk = lax.dynamic_slice_in_dim(cotangent_head, row_start, block_len, 0)
        grad_weights = jnp.einsum('qngd,knd->ngqk', cot_blk, value_win)
        centre = lax.optimization_barrier(jnp.sum(weights * grad_weights, axis=-1, keepdims=True))
        grad_scores = weights * (grad_weights - centre)
        grad_scores = lax.optimization_barrier(grad_scores.astype(jnp.bfloat16)).astype(jnp.float32)
        grad_query = jnp.einsum('ngqk,knd->qngd', grad_scores, key_win) * score_scale
        grad_query = grad_query.astype(jnp.bfloat16).reshape(block_len, QUERY_HEADS * HEAD_DIMENSION)
        key_term = jnp.einsum('ngqk,qngd->knd', grad_scores, query_blk) * score_scale
        value_term = jnp.einsum('ngqk,qngd->knd', rounded, cot_blk)
        key_gradient = lax.dynamic_update_slice_in_dim(key_gradient, lax.dynamic_slice_in_dim(key_gradient, win_start, window, 0) + key_term, win_start, 0)
        value_gradient = lax.dynamic_update_slice_in_dim(value_gradient, lax.dynamic_slice_in_dim(value_gradient, win_start, window, 0) + value_term, win_start, 0)
        return ((key_gradient, value_gradient), grad_query)
    empty_gradient = jnp.zeros((ROWS_PER_GROUP, KEY_VALUE_HEADS, HEAD_DIMENSION), jnp.float32)
    (key_gradient, value_gradient), grad_query = lax.scan(backward, (empty_gradient, empty_gradient), starts)
    grad_query = grad_query.reshape(ROWS_PER_GROUP, QUERY_HEADS * HEAD_DIMENSION)
    key_gradient = key_gradient.astype(jnp.bfloat16).reshape(ROWS_PER_GROUP, KEY_VALUE_HEADS * HEAD_DIMENSION)
    value_gradient = value_gradient.astype(jnp.bfloat16).reshape(ROWS_PER_GROUP, KEY_VALUE_HEADS * HEAD_DIMENSION)
    return (normed_rows, grad_query, key_gradient, value_gradient, gain_part)

def reference(queries, keys, values, cotangent, norm_gain, owner_of_row, arrival, doc_start):
    owner_ids = jnp.arange(N_CTX, dtype=jnp.int32)
    owner_table = owner_of_row.reshape(N_CTX, ROWS_PER_GROUP)
    onehot = (owner_table[:, :, None] == owner_ids[None, None, :]).astype(jnp.int32)
    before = jnp.cumsum(onehot, axis=1) - onehot
    row_rank = lax.optimization_barrier(jnp.sum(before * onehot, axis=2))
    position = owner_ids[:, None] * CAP + row_rank
    arrival_table = arrival.reshape(N_CTX, ROWS_PER_GROUP)
    slot_ids = jnp.arange(ROWS_PER_GROUP, dtype=jnp.int32)
    inverse = jnp.zeros((N_CTX, N_CTX * CAP), jnp.int32).at[owner_ids[:, None], arrival_table].set(slot_ids[None, :])
    slot_of_row = inverse[owner_table, position]
    global_slot = (owner_table * ROWS_PER_GROUP + slot_of_row).reshape(-1)
    row_index = jnp.arange(TOTAL_TOKENS, dtype=jnp.int32)
    row_of_slot = jnp.zeros((TOTAL_TOKENS,), jnp.int32).at[global_slot].set(row_index)

    def gather_slots(matrix):
        return matrix[row_of_slot].reshape(N_CTX, ROWS_PER_GROUP, matrix.shape[1])

    def scatter_rows(matrix):
        return matrix.reshape(TOTAL_TOKENS, matrix.shape[-1])[global_slot]

    def one_owner(inputs):
        return owner_pass(inputs[0], inputs[1], inputs[2], inputs[3], inputs[4], norm_gain)
    normed_o, grad_q, grad_k, grad_v, gain_parts = lax.map(one_owner, (gather_slots(queries), gather_slots(keys), gather_slots(values), gather_slots(cotangent), doc_start.reshape(N_CTX, ROWS_PER_GROUP)))
    return (scatter_rows(normed_o), scatter_rows(grad_q), scatter_rows(grad_k), scatter_rows(grad_v), lax.optimization_barrier(jnp.sum(gain_parts, axis=0)))
```

```python
import functools
import math

import jax
import jax.numpy as jnp
from jax import lax
from jax.experimental import pallas as pl
from jax.experimental.pallas import tpu as pltpu
from jax.sharding import PartitionSpec as P

HEAD = 128
BLOCK = 256
DOC_MAX = 512
HIDDEN = -1e30
VMEM_BYTES = 56 * 1024 * 1024
F32 = jnp.float32
BF16 = jnp.bfloat16


def params(grid_axes):
    return pltpu.CompilerParams(
        dimension_semantics=("arbitrary",) * grid_axes, vmem_limit_bytes=VMEM_BYTES
    )


def whole(shape):
    return pl.BlockSpec(shape, lambda i: (0,) * len(shape))


def row_block(cols, rows=BLOCK):
    return pl.BlockSpec((rows, cols), lambda i: (i, 0))


def as_column(row):
    return jnp.transpose(jnp.broadcast_to(row, (8, row.shape[1])))[:, 0:1]


def dot(a, b):
    return lax.dot_general(a, b, (((1,), (0,)), ((), ())), preferred_element_type=F32)


def dot_nt(a, b):
    return lax.dot_general(a, b, (((1,), (1,)), ((), ())), preferred_element_type=F32)


def cost(flops, nbytes, exps=0):
    return pl.CostEstimate(flops=int(flops), bytes_accessed=int(nbytes), transcendentals=int(exps))


def spread_kernel(target_ref, x_ref, out_ref):
    first = pl.program_id(0) * BLOCK
    place = first + lax.broadcasted_iota(jnp.int32, (BLOCK, target_ref.shape[1]), 0)
    hit = (place == target_ref[...]).astype(F32).astype(BF16)
    out_ref[...] = dot(hit, x_ref[...]).astype(BF16)


def spread_rows(x, target_row, out_rows):
    rows, cols = x.shape
    return pl.pallas_call(
        spread_kernel,
        grid=(out_rows // BLOCK,),
        in_specs=[whole((1, rows)), whole((rows, cols))],
        out_specs=row_block(cols),
        out_shape=jax.ShapeDtypeStruct((out_rows, cols), BF16),
        compiler_params=params(1),
        cost_estimate=cost(2 * rows * cols * out_rows, 2 * cols * (rows + out_rows)),
        name="spread_rows",
    )(target_row, x)


def take_kernel(source_ref, x_ref, out_ref):
    source = as_column(source_ref[...].astype(F32)).astype(jnp.int32)
    lane = lax.broadcasted_iota(jnp.int32, (BLOCK, x_ref.shape[0]), 1)
    hit = (lane == source).astype(F32).astype(BF16)
    out_ref[...] = dot(hit, x_ref[...]).astype(BF16)


def take_rows(x, source_row):
    rows, cols = x.shape
    out_rows = source_row.shape[1]
    return pl.pallas_call(
        take_kernel,
        grid=(out_rows // BLOCK,),
        in_specs=[pl.BlockSpec((1, BLOCK), lambda i: (0, i)), whole((rows, cols))],
        out_specs=row_block(cols),
        out_shape=jax.ShapeDtypeStruct((out_rows, cols), BF16),
        compiler_params=params(1),
        cost_estimate=cost(2 * rows * cols * out_rows, 2 * cols * (rows + out_rows)),
        name="take_rows",
    )(source_row, x)


def key_window(block):
    start = max(0, block * BLOCK - DOC_MAX)
    return start, (block + 1) * BLOCK - start


def window_bias(doc_ref, block):
    start, size = key_window(block)
    key_pos = start + lax.broadcasted_iota(jnp.int32, (size, BLOCK), 0)
    query_pos = block * BLOCK + lax.broadcasted_iota(jnp.int32, (size, BLOCK), 1)
    first_key = doc_ref[0:1, block * BLOCK : (block + 1) * BLOCK]
    return jnp.where((key_pos >= first_key) & (key_pos <= query_pos), 0.0, HIDDEN)


LOG2E = math.log2(math.e)


def forward_kernel(heads, doc_ref, kvq_ref, att_ref, stat_ref, value_t, bias_ref):
    rows = kvq_ref.shape[0]
    scale = HEAD ** (-0.5) * LOG2E
    value_t[...] = jnp.transpose(kvq_ref[:, HEAD : 2 * HEAD].astype(F32)).astype(BF16)
    for block in range(rows // BLOCK):
        start, size = key_window(block)
        q_rows = slice(block * BLOCK, (block + 1) * BLOCK)
        bias_ref[0:size, :] = window_bias(doc_ref, block)
        squares = jnp.zeros((1, BLOCK), F32)
        for head in range(heads):
            lanes = slice(head * HEAD, (head + 1) * HEAD)
            query = kvq_ref[q_rows, (head + 2) * HEAD : (head + 3) * HEAD]
            scores = dot_nt(kvq_ref[start : start + size, 0:HEAD], query) * scale + bias_ref[0:size, :]
            peak = jnp.max(scores, axis=0, keepdims=True)
            raised = jnp.exp2(scores - peak)
            total = jnp.sum(raised, axis=0, keepdims=True)
            weights = (raised * (1.0 / total)).astype(BF16)
            out_t = dot(value_t[:, start : start + size], weights)
            out = out_t.astype(BF16).astype(F32)
            squares = squares + jnp.sum(out * out, axis=0, keepdims=True)
            att_ref[q_rows, lanes] = jnp.transpose(out).astype(BF16)
            stat_ref[head : head + 1, q_rows] = peak + jnp.log2(total)
        stat_ref[7:8, q_rows] = squares


def forward_attention(kvq, doc_row):
    rows, cols = kvq.shape
    heads = cols // HEAD - 2
    pairs = rows * 576 * heads
    return pl.pallas_call(
        functools.partial(forward_kernel, heads),
        out_shape=(
            jax.ShapeDtypeStruct((rows, heads * HEAD), BF16),
            jax.ShapeDtypeStruct((8, rows), F32),
        ),
        scratch_shapes=[pltpu.VMEM((HEAD, rows), BF16), pltpu.VMEM((3 * BLOCK, BLOCK), F32)],
        compiler_params=pltpu.CompilerParams(vmem_limit_bytes=VMEM_BYTES),
        cost_estimate=cost(pairs * 16 * HEAD, 4 * rows * cols, pairs),
        name="forward_attention",
    )(doc_row, kvq)


def pack_normed_kernel(target_ref, att_ref, inv_ref, gain_ref, out_ref, normed):
    @pl.when(pl.program_id(0) == 0)
    def _():
        inv = as_column(inv_ref[...])
        normed[...] = (gain_ref[...] * att_ref[...].astype(F32) * inv).astype(BF16)

    spread_kernel(target_ref, normed, out_ref)


def pack_normed(att, inv_row, gain_row, target_row, out_rows):
    rows, cols = att.shape
    return pl.pallas_call(
        pack_normed_kernel,
        grid=(out_rows // BLOCK,),
        in_specs=[whole((1, rows)), whole((rows, cols)), whole((1, rows)), whole((1, cols))],
        out_specs=row_block(cols),
        out_shape=jax.ShapeDtypeStruct((out_rows, cols), BF16),
        scratch_shapes=[pltpu.VMEM((rows, cols), BF16)],
        compiler_params=params(1),
        cost_estimate=cost(2 * rows * cols * out_rows, 2 * cols * (rows + out_rows)),
        name="pack_normed",
    )(target_row, att, inv_row, gain_row)


def take_cotangent_kernel(source_ref, x_ref, att_ref, inv_ref, gain_ref, out_ref, cross_ref, part_ref):
    take_kernel(source_ref, x_ref, out_ref)
    product = out_ref[...].astype(F32) * att_ref[...].astype(F32)
    cross = jnp.sum(product * gain_ref[...], axis=1, keepdims=True)
    cross_ref[...] = jnp.transpose(jnp.broadcast_to(cross, (BLOCK, HEAD)))[0:1, :]

    @pl.when(pl.program_id(0) == 0)
    def _():
        part_ref[...] = jnp.zeros_like(part_ref)

    part_ref[...] += jnp.sum(product * as_column(inv_ref[...]), axis=0, keepdims=True)


def take_cotangent(received, source_row, att, inv_row, gain_row):
    rows, cols = att.shape
    lanes = pl.BlockSpec((1, BLOCK), lambda i: (0, i))
    return pl.pallas_call(
        take_cotangent_kernel,
        grid=(rows // BLOCK,),
        in_specs=[lanes, whole(received.shape), row_block(cols), lanes, whole((1, cols))],
        out_specs=(row_block(cols), lanes, whole((1, cols))),
        out_shape=(
            jax.ShapeDtypeStruct((rows, cols), BF16),
            jax.ShapeDtypeStruct((1, rows), F32),
            jax.ShapeDtypeStruct((1, cols), F32),
        ),
        compiler_params=params(1),
        cost_estimate=cost(2 * rows * cols * received.shape[0], 2 * cols * (3 * rows)),
        name="take_cotangent",
    )(source_row, received, att, inv_row, gain_row)


def backward_kernel(
    heads, doc_ref, kvq_ref, att_ref, cot_ref, stat_ref, inv_ref, cross_ref, gain_ref,
    out_ref, key_t, key_sum, value_sum, bias_ref,
):
    rows = kvq_ref.shape[0]
    width = heads * HEAD * 8
    scale = HEAD ** (-0.5)
    key_t[...] = jnp.transpose(kvq_ref[:, 0:HEAD].astype(F32)).astype(BF16)
    key_sum[...] = jnp.zeros_like(key_sum)
    value_sum[...] = jnp.zeros_like(value_sum)
    for block in range(rows // BLOCK):
        start, size = key_window(block)
        q_rows = slice(block * BLOCK, (block + 1) * BLOCK)
        keys = slice(start, start + size)
        bias_ref[0:size, :] = window_bias(doc_ref, block)
        inv = as_column(inv_ref[:, q_rows])
        shift = as_column(cross_ref[:, q_rows]) * (inv * inv * inv * (1.0 / width))
        for head in range(heads):
            lanes = slice(head * HEAD, (head + 1) * HEAD)
            wide = slice((head + 2) * HEAD, (head + 3) * HEAD)
            query = kvq_ref[q_rows, wide]
            grad = (
                gain_ref[:, lanes] * cot_ref[q_rows, lanes].astype(F32) * inv
                - att_ref[q_rows, lanes].astype(F32) * shift
            ).astype(BF16)
            scores = dot_nt(kvq_ref[keys, 0:HEAD], query) * (scale * LOG2E) + bias_ref[0:size, :]
            weights = jnp.exp2(scores - stat_ref[head : head + 1, q_rows])
            grad_weights = dot_nt(kvq_ref[keys, HEAD : 2 * HEAD], grad)
            centre = jnp.sum(weights * grad_weights, axis=0, keepdims=True)
            grad_scores = (weights * (grad_weights - centre)).astype(BF16)
            key_sum[keys, :] += dot(grad_scores, query)
            value_sum[keys, :] += dot(weights.astype(BF16), grad)
            grad_query = dot(key_t[:, keys], grad_scores) * scale
            out_ref[q_rows, wide] = jnp.transpose(grad_query).astype(BF16)
    out_ref[:, 0:HEAD] = (key_sum[...] * scale).astype(BF16)
    out_ref[:, HEAD : 2 * HEAD] = value_sum[...].astype(BF16)


def backward_attention(kvq, doc_row, att, cot, stats, inv_row, cross_row, gain_row):
    rows, cols = kvq.shape
    heads = cols // HEAD - 2
    pairs = rows * 576 * heads
    return pl.pallas_call(
        functools.partial(backward_kernel, heads),
        out_shape=jax.ShapeDtypeStruct((rows, cols), BF16),
        scratch_shapes=[
            pltpu.VMEM((HEAD, rows), BF16),
            pltpu.VMEM((rows, HEAD), F32),
            pltpu.VMEM((rows, HEAD), F32),
            pltpu.VMEM((3 * BLOCK, BLOCK), F32),
        ],
        compiler_params=pltpu.CompilerParams(vmem_limit_bytes=VMEM_BYTES),
        cost_estimate=cost(pairs * 30 * HEAD, 8 * rows * cols, pairs),
        name="backward_attention",
    )(doc_row, kvq, att, cot, stats, inv_row, cross_row, gain_row)


def sum_over(x, axis):
    size = lax.axis_size(axis)
    step = 1
    while step < size:
        x = x + lax.ppermute(x, axis, [(i, i ^ step) for i in range(size)])
        step *= 2
    return x


def shifted(axis, by):
    size = lax.axis_size(axis)
    return [(i, (i + by) % size) for i in range(size)]


def exchange(x, axis):
    return lax.all_to_all(x, axis, split_axis=0, concat_axis=0, tiled=True)


def per_device(queries, keys, values, cotangent, norm_gain, owner_of_row, arrival, doc_start):
    tok = queries.shape[0]
    uly = lax.axis_size("uly")
    ctx = lax.axis_size("ctx")
    rows = tok * uly
    capacity = 2 * rows // ctx
    sent = ctx * capacity
    width = queries.shape[1]
    feat = width // uly
    me = lax.axis_index("uly")

    with jax.named_scope("plan"):
        owner_ids = jnp.arange(ctx, dtype=jnp.int32)
        onehot = (owner_of_row[:, None] == owner_ids[None, :]).astype(BF16)
        row_ids = jnp.arange(rows, dtype=jnp.int32)
        earlier = (row_ids[None, :] < row_ids[:, None]).astype(BF16)
        before = dot(earlier, onehot)
        rank = jnp.sum(before * onehot.astype(F32), axis=1).astype(jnp.int32)
        position = (owner_of_row * capacity + rank)[None, :]
        by_shift = position.reshape(uly, tok)[(me - jnp.arange(uly)) % uly].reshape(1, rows)
        arrival_row = arrival[None, :]
        doc_row = doc_start[None, :]
        gain_row = lax.dynamic_slice_in_dim(norm_gain, me * feat, feat)[None, :]

    with jax.named_scope("rows_in"):
        kvq = jnp.concatenate(
            [
                keys.reshape(tok, uly, -1),
                values.reshape(tok, uly, -1),
                queries.reshape(tok, uly, feat),
            ],
            axis=2,
        ).transpose(1, 0, 2)
        kvq = exchange(kvq, "uly").reshape(rows, -1)
        cols = kvq.shape[1]
        kvq = spread_rows(kvq, position, sent)
        kvq = exchange(kvq.reshape(ctx, capacity, cols), "ctx").reshape(sent, cols)

    with jax.named_scope("cotangent_in"):
        blocks = []
        for shift in range(uly):
            block = lax.dynamic_slice_in_dim(cotangent, (me + shift) % uly * feat, feat, axis=1)
            blocks.append(lax.ppermute(block, "uly", shifted("uly", shift)) if shift else block)
        cot = spread_rows(jnp.concatenate(blocks, axis=0), by_shift, sent)
        cot = exchange(cot.reshape(ctx, capacity, feat), "ctx").reshape(sent, feat)

    with jax.named_scope("forward"):
        kvq = take_rows(kvq, arrival_row)
        att, stats = forward_attention(kvq, doc_row)
        square_sum = sum_over(stats[7:8, :], "uly")
        inv_root = lax.rsqrt(square_sum / width + 1e-06)

    with jax.named_scope("normed_out"):
        normed = pack_normed(att, inv_root, gain_row, arrival_row, sent)
        normed = exchange(normed.reshape(ctx, capacity, feat), "ctx").reshape(sent, feat)

    with jax.named_scope("backward"):
        cot, cross, gain_part = take_cotangent(cot, arrival_row, att, inv_root, gain_row)
        cross = sum_over(cross, "uly")
        grads = backward_attention(kvq, doc_row, att, cot, stats, inv_root, cross, gain_row)

    with jax.named_scope("grads_out"):
        grads = spread_rows(grads, arrival_row, sent)
        grads, normed = lax.optimization_barrier((grads, normed))
        grads = exchange(grads.reshape(ctx, capacity, cols), "ctx").reshape(sent, cols)

    with jax.named_scope("normed_rows"):
        normed = take_rows(normed, position).reshape(uly, tok, feat)
        normed_out = jnp.zeros((tok, width), BF16)
        for shift in range(uly):
            block = lax.dynamic_index_in_dim(normed, (me + shift) % uly, 0, keepdims=False)
            block = lax.ppermute(block, "uly", shifted("uly", shift)) if shift else block
            normed_out = lax.dynamic_update_slice_in_dim(
                normed_out, block, (me - shift) % uly * feat, axis=1
            )

    with jax.named_scope("grad_rows"):
        grads, normed_out = lax.optimization_barrier((grads, normed_out))
        grads = take_rows(grads, position).reshape(uly, tok, cols)
    with jax.named_scope("gain_out"):
        gain_part, grads = lax.optimization_barrier((gain_part, grads))
        gain_total = sum_over(gain_part, "ctx")
        grad_gain = jnp.zeros((1, width), F32)
        for shift in range(uly):
            block = lax.ppermute(gain_total, "uly", shifted("uly", shift)) if shift else gain_total
            grad_gain = lax.dynamic_update_slice_in_dim(
                grad_gain, block, (me - shift) % uly * feat, axis=1
            )

    with jax.named_scope("grad_cols"):
        grads = exchange(grads, "uly").transpose(1, 0, 2)
        grad_keys = grads[:, :, 0:HEAD].reshape(tok, -1)
        grad_values = grads[:, :, HEAD : 2 * HEAD].reshape(tok, -1)
        grad_queries = grads[:, :, 2 * HEAD :].reshape(tok, width)
    return normed_out, grad_queries, grad_keys, grad_values, grad_gain.reshape(width)


def solution(mesh):
    split = P(("ctx", "uly"), None)
    plan = P("ctx")
    return jax.shard_map(
        per_device,
        mesh=mesh,
        in_specs=(split, split, split, split, P(), plan, plan, plan),
        out_specs=(split, split, split, split, P()),
        check_vma=False,
    )
```

```python
import functools
import math

import jax
import jax.numpy as jnp
from jax import lax
from jax.experimental import pallas as pl
from jax.experimental.pallas import tpu as pltpu
from jax.sharding import PartitionSpec as P

HEAD = 128
BLOCK = 256
DOC_MAX = 512
HIDDEN = -1e30
VMEM_BYTES = 56 * 1024 * 1024
F32 = jnp.float32
BF16 = jnp.bfloat16


def params(grid_axes):
    return pltpu.CompilerParams(
        dimension_semantics=("arbitrary",) * grid_axes, vmem_limit_bytes=VMEM_BYTES
    )


def whole(shape):
    return pl.BlockSpec(shape, lambda i: (0,) * len(shape))


def row_block(cols, rows=BLOCK):
    return pl.BlockSpec((rows, cols), lambda i: (i, 0))


def as_column(row):
    return jnp.transpose(jnp.broadcast_to(row, (8, row.shape[1])))[:, 0:1]


def dot(a, b):
    return lax.dot_general(a, b, (((1,), (0,)), ((), ())), preferred_element_type=F32)


def dot_nt(a, b):
    return lax.dot_general(a, b, (((1,), (1,)), ((), ())), preferred_element_type=F32)


def cost(flops, nbytes, exps=0):
    return pl.CostEstimate(flops=int(flops), bytes_accessed=int(nbytes), transcendentals=int(exps))


def spread_kernel(target_ref, x_ref, out_ref):
    first = pl.program_id(0) * BLOCK
    place = first + lax.broadcasted_iota(jnp.int32, (BLOCK, target_ref.shape[1]), 0)
    hit = (place == target_ref[...]).astype(F32).astype(BF16)
    out_ref[...] = dot(hit, x_ref[...]).astype(BF16)


def spread_rows(x, target_row, out_rows):
    rows, cols = x.shape
    return pl.pallas_call(
        spread_kernel,
        grid=(out_rows // BLOCK,),
        in_specs=[whole((1, rows)), whole((rows, cols))],
        out_specs=row_block(cols),
        out_shape=jax.ShapeDtypeStruct((out_rows, cols), BF16),
        compiler_params=params(1),
        cost_estimate=cost(2 * rows * cols * out_rows, 2 * cols * (rows + out_rows)),
        name="spread_rows",
    )(target_row, x)


def take_kernel(source_ref, x_ref, out_ref):
    source = as_column(source_ref[...].astype(F32)).astype(jnp.int32)
    lane = lax.broadcasted_iota(jnp.int32, (BLOCK, x_ref.shape[0]), 1)
    hit = (lane == source).astype(F32).astype(BF16)
    out_ref[...] = dot(hit, x_ref[...]).astype(BF16)


def take_rows(x, source_row):
    rows, cols = x.shape
    out_rows = source_row.shape[1]
    return pl.pallas_call(
        take_kernel,
        grid=(out_rows // BLOCK,),
        in_specs=[pl.BlockSpec((1, BLOCK), lambda i: (0, i)), whole((rows, cols))],
        out_specs=row_block(cols),
        out_shape=jax.ShapeDtypeStruct((out_rows, cols), BF16),
        compiler_params=params(1),
        cost_estimate=cost(2 * rows * cols * out_rows, 2 * cols * (rows + out_rows)),
        name="take_rows",
    )(source_row, x)


def key_window(block):
    start = max(0, block * BLOCK - DOC_MAX)
    return start, (block + 1) * BLOCK - start


def window_bias(doc_ref, block):
    start, size = key_window(block)
    key_pos = start + lax.broadcasted_iota(jnp.int32, (size, BLOCK), 0)
    query_pos = block * BLOCK + lax.broadcasted_iota(jnp.int32, (size, BLOCK), 1)
    first_key = doc_ref[0:1, block * BLOCK : (block + 1) * BLOCK]
    return jnp.where((key_pos >= first_key) & (key_pos <= query_pos), 0.0, HIDDEN)


LOG2E = math.log2(math.e)


def forward_kernel(heads, doc_ref, kvq_ref, att_ref, stat_ref, value_t, bias_ref):
    rows = kvq_ref.shape[0]
    scale = HEAD ** (-0.5) * LOG2E
    value_t[...] = jnp.transpose(kvq_ref[:, HEAD : 2 * HEAD].astype(F32)).astype(BF16)
    for block in range(rows // BLOCK):
        start, size = key_window(block)
        q_rows = slice(block * BLOCK, (block + 1) * BLOCK)
        bias_ref[0:size, :] = window_bias(doc_ref, block)
        squares = jnp.zeros((1, BLOCK), F32)
        for head in range(heads):
            lanes = slice(head * HEAD, (head + 1) * HEAD)
            query = kvq_ref[q_rows, (head + 2) * HEAD : (head + 3) * HEAD]
            scores = dot_nt(kvq_ref[start : start + size, 0:HEAD], query) * scale + bias_ref[0:size, :]
            peak = jnp.max(scores, axis=0, keepdims=True)
            raised = jnp.exp2(scores - peak)
            total = jnp.sum(raised, axis=0, keepdims=True)
            weights = (raised * (1.0 / total)).astype(BF16)
            out_t = dot(value_t[:, start : start + size], weights)
            out = out_t.astype(BF16).astype(F32)
            squares = squares + jnp.sum(out * out, axis=0, keepdims=True)
            att_ref[q_rows, lanes] = jnp.transpose(out).astype(BF16)
            stat_ref[head : head + 1, q_rows] = peak + jnp.log2(total)
        stat_ref[7:8, q_rows] = squares


def forward_attention(kvq, doc_row):
    rows, cols = kvq.shape
    heads = cols // HEAD - 2
    pairs = rows * 576 * heads
    return pl.pallas_call(
        functools.partial(forward_kernel, heads),
        out_shape=(
            jax.ShapeDtypeStruct((rows, heads * HEAD), BF16),
            jax.ShapeDtypeStruct((8, rows), F32),
        ),
        scratch_shapes=[pltpu.VMEM((HEAD, rows), BF16), pltpu.VMEM((3 * BLOCK, BLOCK), F32)],
        compiler_params=pltpu.CompilerParams(vmem_limit_bytes=VMEM_BYTES),
        cost_estimate=cost(pairs * 16 * HEAD, 4 * rows * cols, pairs),
        name="forward_attention",
    )(doc_row, kvq)


def pack_normed_kernel(target_ref, att_ref, inv_ref, gain_ref, out_ref, normed):
    @pl.when(pl.program_id(0) == 0)
    def _():
        inv = as_column(inv_ref[...])
        normed[...] = (gain_ref[...] * att_ref[...].astype(F32) * inv).astype(BF16)

    spread_kernel(target_ref, normed, out_ref)


def pack_normed(att, inv_row, gain_row, target_row, out_rows):
    rows, cols = att.shape
    return pl.pallas_call(
        pack_normed_kernel,
        grid=(out_rows // BLOCK,),
        in_specs=[whole((1, rows)), whole((rows, cols)), whole((1, rows)), whole((1, cols))],
        out_specs=row_block(cols),
        out_shape=jax.ShapeDtypeStruct((out_rows, cols), BF16),
        scratch_shapes=[pltpu.VMEM((rows, cols), BF16)],
        compiler_params=params(1),
        cost_estimate=cost(2 * rows * cols * out_rows, 2 * cols * (rows + out_rows)),
        name="pack_normed",
    )(target_row, att, inv_row, gain_row)


def take_cotangent_kernel(source_ref, x_ref, att_ref, inv_ref, gain_ref, out_ref, cross_ref, part_ref):
    take_kernel(source_ref, x_ref, out_ref)
    cotangent_sums(att_ref, inv_ref, gain_ref, out_ref, cross_ref, part_ref)


def cotangent_sums(att_ref, inv_ref, gain_ref, out_ref, cross_ref, part_ref):
    product = out_ref[...].astype(F32) * att_ref[...].astype(F32)
    cross = jnp.sum(product * gain_ref[...], axis=1, keepdims=True)
    cross_ref[...] = jnp.transpose(jnp.broadcast_to(cross, (cross.shape[0], HEAD)))[0:1, :]

    @pl.when(pl.program_id(0) == 0)
    def _():
        part_ref[...] = jnp.zeros_like(part_ref)

    part_ref[...] += jnp.sum(product * as_column(inv_ref[...]), axis=0, keepdims=True)


def take_cotangent(received, source_row, att, inv_row, gain_row):
    rows, cols = att.shape
    lanes = pl.BlockSpec((1, BLOCK), lambda i: (0, i))
    return pl.pallas_call(
        take_cotangent_kernel,
        grid=(rows // BLOCK,),
        in_specs=[lanes, whole(received.shape), row_block(cols), lanes, whole((1, cols))],
        out_specs=(row_block(cols), lanes, whole((1, cols))),
        out_shape=(
            jax.ShapeDtypeStruct((rows, cols), BF16),
            jax.ShapeDtypeStruct((1, rows), F32),
            jax.ShapeDtypeStruct((1, cols), F32),
        ),
        compiler_params=params(1),
        cost_estimate=cost(2 * rows * cols * received.shape[0], 2 * cols * (3 * rows)),
        name="take_cotangent",
    )(source_row, received, att, inv_row, gain_row)


def backward_kernel(
    heads, doc_ref, kvq_ref, att_ref, cot_ref, stat_ref, inv_ref, cross_ref, gain_ref,
    out_ref, key_t, key_sum, value_sum, bias_ref,
):
    rows = kvq_ref.shape[0]
    width = heads * HEAD * 8
    scale = HEAD ** (-0.5)
    key_t[...] = jnp.transpose(kvq_ref[:, 0:HEAD].astype(F32)).astype(BF16)
    key_sum[...] = jnp.zeros_like(key_sum)
    value_sum[...] = jnp.zeros_like(value_sum)
    for block in range(rows // BLOCK):
        start, size = key_window(block)
        q_rows = slice(block * BLOCK, (block + 1) * BLOCK)
        keys = slice(start, start + size)
        bias_ref[0:size, :] = window_bias(doc_ref, block)
        inv = as_column(inv_ref[:, q_rows])
        shift = as_column(cross_ref[:, q_rows]) * (inv * inv * inv * (1.0 / width))
        for head in range(heads):
            lanes = slice(head * HEAD, (head + 1) * HEAD)
            wide = slice((head + 2) * HEAD, (head + 3) * HEAD)
            query = kvq_ref[q_rows, wide]
            grad = (
                gain_ref[:, lanes] * cot_ref[q_rows, lanes].astype(F32) * inv
                - att_ref[q_rows, lanes].astype(F32) * shift
            ).astype(BF16)
            scores = dot_nt(kvq_ref[keys, 0:HEAD], query) * (scale * LOG2E) + bias_ref[0:size, :]
            weights = jnp.exp2(scores - stat_ref[head : head + 1, q_rows])
            grad_weights = dot_nt(kvq_ref[keys, HEAD : 2 * HEAD], grad)
            centre = jnp.sum(weights * grad_weights, axis=0, keepdims=True)
            grad_scores = (weights * (grad_weights - centre)).astype(BF16)
            key_sum[keys, :] += dot(grad_scores, query)
            value_sum[keys, :] += dot(weights.astype(BF16), grad)
            grad_query = dot(key_t[:, keys], grad_scores) * scale
            out_ref[q_rows, wide] = jnp.transpose(grad_query).astype(BF16)
    out_ref[:, 0:HEAD] = (key_sum[...] * scale).astype(BF16)
    out_ref[:, HEAD : 2 * HEAD] = value_sum[...].astype(BF16)


def backward_attention(kvq, doc_row, att, cot, stats, inv_row, cross_row, gain_row):
    rows, cols = kvq.shape
    heads = cols // HEAD - 2
    pairs = rows * 576 * heads
    return pl.pallas_call(
        functools.partial(backward_kernel, heads),
        out_shape=jax.ShapeDtypeStruct((rows, cols), BF16),
        scratch_shapes=[
            pltpu.VMEM((HEAD, rows), BF16),
            pltpu.VMEM((rows, HEAD), F32),
            pltpu.VMEM((rows, HEAD), F32),
            pltpu.VMEM((3 * BLOCK, BLOCK), F32),
        ],
        compiler_params=pltpu.CompilerParams(vmem_limit_bytes=VMEM_BYTES),
        cost_estimate=cost(pairs * 30 * HEAD, 8 * rows * cols, pairs),
        name="backward_attention",
    )(doc_row, kvq, att, cot, stats, inv_row, cross_row, gain_row)


def sum_over(x, axis):
    size = lax.axis_size(axis)
    step = 1
    while step < size:
        x = x + lax.ppermute(x, axis, [(i, i ^ step) for i in range(size)])
        step *= 2
    return x


def shifted(axis, by):
    size = lax.axis_size(axis)
    return [(i, (i + by) % size) for i in range(size)]


def exchange(x, axis):
    return lax.all_to_all(x, axis, split_axis=0, concat_axis=0, tiled=True)


SLOTS = 32
TAIL = 16


def tile(n):
    return slice(n * HEAD, (n + 1) * HEAD)


PLACED = 512


def one_hot(flags):
    return flags.astype(F32).astype(BF16)


def iota(shape, dim):
    return lax.broadcasted_iota(jnp.int32, shape, dim)


def constant(shape):
    return pl.BlockSpec(shape, lambda i, *_: (0,) * len(shape))


def cube(count, chunk_rows):
    return pl.BlockSpec((count, chunk_rows, HEAD), lambda i, *_: (i, 0, 0))


def spread_body(x_ref, target_ref, out_ref, chunks):
    place = pl.program_id(0) * PLACED + iota((PLACED, target_ref.shape[1]), 0)
    found = dot(one_hot(place == target_ref[...]), x_ref[...]).astype(BF16)
    for n in range(chunks):
        out_ref[:, n * SLOTS : (n + 1) * SLOTS, :] = found[:, tile(n)].reshape(-1, SLOTS, HEAD)


def plan_kernel(ctx, capacity, owner_ref, place_ref, via_ref, position_ref, count_ref):
    owner = owner_ref[...]
    rows = owner.shape[1]
    mine = iota((ctx, rows), 0) == owner
    mine_wide = mine.astype(F32)
    earlier = one_hot(iota((rows, rows), 0) < iota((rows, rows), 1))
    rank = jnp.sum(dot(mine_wide.astype(BF16), earlier) * mine_wide, axis=0, keepdims=True)
    counts = jnp.sum(mine_wide, axis=1, keepdims=True)
    beyond = jnp.broadcast_to(jnp.maximum(counts - SLOTS, 0.0), (ctx, HEAD))
    lower = one_hot(iota((ctx, ctx), 1) < iota((ctx, ctx), 0))
    begin = dot(lower, beyond.astype(BF16))[:, 0:1]
    via = jnp.sum(begin * mine_wide, axis=0, keepdims=True) + rank - SLOTS
    rank = rank.astype(jnp.int32)
    inside = rank < SLOTS
    place_ref[...] = jnp.where(inside, owner * SLOTS + rank, -1)
    via_ref[...] = jnp.where(inside, -1, via.astype(jnp.int32))
    position_ref[...] = owner * capacity + rank
    padded = jnp.concatenate([jnp.broadcast_to(counts, (ctx, HEAD)), jnp.zeros((HEAD - ctx, HEAD), F32)], axis=0)
    count_ref[...] = jnp.transpose(padded)[0:TAIL, :].astype(BF16)


def plan_rows(owner_row, ctx, capacity):
    rows = owner_row.shape[1]
    line = jax.ShapeDtypeStruct((1, rows), jnp.int32)
    return pl.pallas_call(
        functools.partial(plan_kernel, ctx, capacity),
        out_shape=(line, line, line, jax.ShapeDtypeStruct((TAIL, HEAD), BF16)),
        compiler_params=pltpu.CompilerParams(vmem_limit_bytes=VMEM_BYTES),
        cost_estimate=cost(2 * rows * rows * ctx, 8 * rows),
        name="plan_rows",
    )(owner_row)


def choice_kernel(
    capacity, here_ref, table_ref, arrival_ref, fits_ref, source_ref, ahead_ref, back_ref
):
    ctx = table_ref.shape[0]
    here = here_ref[0]
    beyond = jnp.maximum(table_ref[:, 0:HEAD].astype(F32) - SLOTS, 0.0)
    before = one_hot(iota((HEAD, HEAD), 0) < iota((HEAD, HEAD), 1))
    begin = dot(beyond.astype(BF16), before)
    end = begin + beyond
    most = jnp.max(jnp.sum(beyond, axis=1, keepdims=True), axis=0, keepdims=True)
    worst = jnp.zeros((1, HEAD), F32)
    for n in range(ctx):
        led = ((begin <= n) & (n < end)).astype(F32)
        worst = jnp.maximum(worst, jnp.sum(led, axis=0, keepdims=True))
    worst = jnp.max(worst, axis=1, keepdims=True)
    fits = (most <= ctx) & (worst <= 1.0)
    fits_ref[...] = jnp.broadcast_to(fits.astype(jnp.int32), fits_ref.shape)
    number = here.astype(F32)
    led = ((begin <= number) & (number < end)).astype(F32)
    group = iota((ctx, HEAD), 0).astype(F32)
    lane = iota((ctx, HEAD), 1)
    ahead_ref[...] = jnp.sum(led * group, axis=0, keepdims=True).astype(jnp.int32)
    back = jnp.sum(led * lane.astype(F32), axis=1, keepdims=True)
    back_ref[...] = jnp.broadcast_to(back, (ctx, HEAD)).astype(jnp.int32)
    begin_here = jnp.sum(jnp.where(lane == here, begin, 0.0), axis=1, keepdims=True)
    arrival = arrival_ref[...]
    rows = arrival.shape[1]
    source_group = arrival // capacity
    rank = arrival - source_group * capacity
    passed = jnp.sum(
        jnp.where(iota((ctx, rows), 0) == source_group, begin_here, 0.0), axis=0, keepdims=True
    ).astype(jnp.int32)
    source_ref[...] = jnp.where(
        rank < SLOTS, source_group * SLOTS + rank, ctx * SLOTS + passed + rank - SLOTS
    )


def choose(here, table, arrival_row, capacity):
    ctx = table.shape[0]
    return pl.pallas_call(
        functools.partial(choice_kernel, capacity),
        grid_spec=pltpu.PrefetchScalarGridSpec(
            num_scalar_prefetch=1,
            grid=(1,),
            in_specs=[constant(table.shape), constant(arrival_row.shape)],
            out_specs=[
                constant((8, HEAD)), constant(arrival_row.shape), constant((1, HEAD)), constant((ctx, HEAD)),
            ],
        ),
        out_shape=[
            jax.ShapeDtypeStruct((8, HEAD), jnp.int32),
            jax.ShapeDtypeStruct(arrival_row.shape, jnp.int32),
            jax.ShapeDtypeStruct((1, HEAD), jnp.int32),
            jax.ShapeDtypeStruct((ctx, HEAD), jnp.int32),
        ],
        compiler_params=params(1),
        cost_estimate=cost(1e6, 1e5),
        name="choose",
    )(here, table, arrival_row)


def split_kernel(size, me_ref, via_ref, key_ref, value_ref, query_ref, cot_ref, *outs):
    blocks, picked = outs[0:size], outs[size:]
    peers = picked[0].shape[0]
    pick = one_hot(iota((peers, via_ref.shape[1]), 0) == via_ref[...])
    shift = pl.program_id(0)
    cols = blocks[0].shape[1]
    for turn in range(size):

        @pl.when(shift == turn)
        def _():
            blocks[turn][:, 0:HEAD] = key_ref[...]
            blocks[turn][:, HEAD : 2 * HEAD] = value_ref[...]
            blocks[turn][:, 2 * HEAD :] = query_ref[...]
            picked[turn][:, 0:HEAD] = dot(pick, key_ref[...]).astype(BF16)
            picked[turn][:, HEAD : 2 * HEAD] = dot(pick, value_ref[...]).astype(BF16)
            picked[turn][:, 2 * HEAD : cols] = dot(pick, query_ref[...]).astype(BF16)
            picked[turn][:, cols:] = dot(pick, cot_ref[...]).astype(BF16)


def split_rows(me, via_row, keys, values, queries, cotangent, size, peers):
    tok, width = queries.shape
    feat = width // size
    cols = feat + 2 * HEAD

    def column(width):
        return pl.BlockSpec((tok, width), lambda i, me_ref: (0, (me_ref[0] + i) % size))

    return pl.pallas_call(
        functools.partial(split_kernel, size),
        grid_spec=pltpu.PrefetchScalarGridSpec(
            num_scalar_prefetch=1,
            grid=(size,),
            in_specs=[
                pl.BlockSpec((1, tok), lambda i, me_ref: (0, me_ref[0])),
                column(HEAD), column(HEAD), column(feat), column(feat),
            ],
            out_specs=[constant((tok, cols))] * size + [constant((peers, cols + feat))] * size,
        ),
        out_shape=[jax.ShapeDtypeStruct((tok, cols), BF16)] * size
        + [jax.ShapeDtypeStruct((peers, cols + feat), BF16)] * size,
        compiler_params=params(1),
        cost_estimate=cost(2 * peers * tok * 2 * width, 8 * tok * width),
        name="split_rows",
    )(me, via_row, keys, values, queries, cotangent)


def join_kernel(count_ref, *refs):
    *picked, out_ref = refs
    total = picked[0][...].astype(F32)
    for ref in picked[1:]:
        total = total + ref[...].astype(F32)
    peers = total.shape[0]
    copies = one_hot(iota((peers * TAIL, peers), 0) // TAIL == iota((peers * TAIL, peers), 1))
    found = dot(copies, total.astype(BF16))
    turn = iota((peers * TAIL, HEAD), 0) % TAIL
    chunks = jnp.zeros((peers * TAIL, HEAD), F32)
    for n in range(TAIL):
        chunks = jnp.where(turn == n, found[:, tile(n)], chunks)
    out_ref[:, 0:TAIL, :] = chunks.astype(BF16).reshape(peers, TAIL, HEAD)
    out_ref[:, TAIL:, :] = jnp.broadcast_to(count_ref[...][None], (peers, TAIL, HEAD))


def join_picked(counts, picked):
    peers = picked[0].shape[0]
    return pl.pallas_call(
        join_kernel,
        out_shape=jax.ShapeDtypeStruct((peers, 2 * TAIL, HEAD), BF16),
        compiler_params=pltpu.CompilerParams(vmem_limit_bytes=VMEM_BYTES),
        cost_estimate=cost(1e7, 2e6),
        name="join_picked",
    )(counts, *picked)


def pack_kernel(size, chunks, me_ref, target_ref, *refs):
    blocks, tail_ref, out_ref, rows = refs[0:size], refs[size : len(refs) - 2], refs[-2], refs[-1]

    @pl.when(pl.program_id(0) == 0)
    def _():
        tok = blocks[0].shape[0]
        for shift in range(size):
            first = pl.multiple_of((me_ref[0] + size - shift) % size * tok, tok)
            rows[pl.ds(first, tok), :] = blocks[shift][...]

    spread_body(rows, target_ref, out_ref, chunks)
    if tail_ref:
        out_ref[:, chunks * SLOTS :, :] = tail_ref[0][...]


def pack_rows(me, blocks, target_row, peers, tail=None):
    size = len(blocks)
    tok, cols = blocks[0].shape
    rows = tok * size
    chunks = cols // HEAD
    step = PLACED // SLOTS
    depth = chunks * SLOTS + (TAIL if tail is not None else 0)
    tails = () if tail is None else (tail,)
    return pl.pallas_call(
        functools.partial(pack_kernel, size, chunks),
        grid_spec=pltpu.PrefetchScalarGridSpec(
            num_scalar_prefetch=1,
            grid=(peers // step,),
            in_specs=[constant((1, rows))]
            + [constant((tok, cols))] * size
            + [cube(step, TAIL)] * len(tails),
            out_specs=cube(step, depth),
            scratch_shapes=[pltpu.VMEM((rows, cols), BF16)],
        ),
        out_shape=jax.ShapeDtypeStruct((peers, depth, HEAD), BF16),
        compiler_params=params(1),
        cost_estimate=cost(2 * rows * cols * peers * SLOTS, 4 * rows * cols),
        name="pack_rows",
    )(me, target_row, *blocks, *tails)


def pack_normed_slots_kernel(chunks, target_ref, att_ref, inv_ref, gain_ref, out_ref, normed_ref):
    @pl.when(pl.program_id(0) == 0)
    def _():
        inv = as_column(inv_ref[...])
        normed_ref[...] = (gain_ref[...] * att_ref[...].astype(F32) * inv).astype(BF16)

    spread_body(normed_ref, target_ref, out_ref, chunks)


def pack_normed_slots(att, inv_row, gain_row, target_row, peers):
    rows, cols = att.shape
    chunks = cols // HEAD
    step = PLACED // SLOTS
    return pl.pallas_call(
        functools.partial(pack_normed_slots_kernel, chunks),
        grid=(peers // step,),
        in_specs=[whole((1, rows)), whole((rows, cols)), whole((1, rows)), whole((1, cols))],
        out_specs=(cube(step, chunks * SLOTS), whole((rows, cols))),
        out_shape=(
            jax.ShapeDtypeStruct((peers, chunks * SLOTS, HEAD), BF16),
            jax.ShapeDtypeStruct((rows, cols), BF16),
        ),
        compiler_params=params(1),
        cost_estimate=cost(2 * rows * cols * peers * SLOTS, 6 * rows * cols),
        name="pack_normed_slots",
    )(target_row, att, inv_row, gain_row)


def pack_grads_kernel(target_ref, grads_ref, normed_ref, part_ref, out_ref):
    chunks = grads_ref.shape[1] // HEAD
    more = normed_ref.shape[1] // HEAD
    peers = pl.num_programs(0) * (PLACED // SLOTS)
    spread_body(grads_ref, target_ref, out_ref, chunks)
    step = out_ref.shape[0]
    row = iota((step * TAIL, target_ref.shape[1]), 0)
    place = peers * SLOTS + pl.program_id(0) * step + row // TAIL
    hit = one_hot(place == target_ref[...])
    found = (dot(hit, grads_ref[...]), dot(hit, normed_ref[...]))
    turn = iota((step * TAIL, HEAD), 0) % TAIL
    tail = jnp.zeros((step * TAIL, HEAD), F32)
    for n in range(chunks + more):
        piece = found[0][:, tile(n)] if n < chunks else found[1][:, tile(n - chunks)]
        tail = jnp.where(turn == n, piece, tail)
    at = chunks * SLOTS
    out_ref[:, at : at + TAIL, :] = tail.astype(BF16).reshape(step, TAIL, HEAD)
    out_ref[:, at + TAIL :, :] = jnp.broadcast_to(part_ref[...][None], (step, TAIL, HEAD))


def pack_grads(grads, normed, part, target_row, peers):
    rows, cols = grads.shape
    step = PLACED // SLOTS
    depth = cols // HEAD * SLOTS + 2 * TAIL
    return pl.pallas_call(
        pack_grads_kernel,
        grid=(peers // step,),
        in_specs=[whole((1, rows)), whole(grads.shape), whole(normed.shape), whole(part.shape)],
        out_specs=cube(step, depth),
        out_shape=jax.ShapeDtypeStruct((peers, depth, HEAD), BF16),
        compiler_params=params(1),
        cost_estimate=cost(4 * rows * cols * peers * SLOTS, 6 * rows * cols),
        name="pack_grads",
    )(target_row, grads, normed, part)


def lay_rows(chunks, first_tail, received_ref, tail_ref, laid):
    peers = received_ref.shape[0]
    main = peers * SLOTS
    for n in range(chunks):
        laid[0:main, tile(n)] = received_ref[:, n * SLOTS : (n + 1) * SLOTS, :].reshape(main, HEAD)
    if tail_ref is not None:
        tails = tail_ref[...].reshape(peers * TAIL, HEAD)
        peer = iota((peers, peers * TAIL), 0)
        lane = iota((peers, peers * TAIL), 1)
        for n in range(chunks):
            pick = one_hot(lane == peer * TAIL + first_tail + n)
            laid[main : main + peers, tile(n)] = dot(pick, tails).astype(BF16)
        laid[main + peers :, :] = jnp.zeros_like(laid[main + peers :, :])


def find_rows(source, laid):
    source = as_column(source.astype(F32)).astype(jnp.int32)
    lane = iota((source.shape[0], laid.shape[0]), 1)
    return dot(one_hot(lane == source), laid[...]).astype(BF16)


def unpack_kernel(chunks, source_ref, received_ref, tail_ref, out_ref, laid):
    @pl.when(pl.program_id(0) == 0)
    def _():
        lay_rows(chunks, 0, received_ref, tail_ref, laid)

    out_ref[...] = find_rows(source_ref[...], laid)


def unpack_rows(received, source_row, chunks, tail):
    peers = received.shape[0]
    rows = source_row.shape[1]
    cols = chunks * HEAD
    laid_rows = peers * SLOTS + HEAD
    return pl.pallas_call(
        functools.partial(unpack_kernel, chunks),
        grid=(rows // PLACED,),
        in_specs=[
            pl.BlockSpec((1, PLACED), lambda i: (0, i)), whole(received.shape), whole(tail.shape),
        ],
        out_specs=row_block(cols, PLACED),
        out_shape=jax.ShapeDtypeStruct((rows, cols), BF16),
        scratch_shapes=[pltpu.VMEM((laid_rows, cols), BF16)],
        compiler_params=params(1),
        cost_estimate=cost(2 * rows * cols * laid_rows, 4 * rows * cols),
        name="unpack_rows",
    )(source_row, received, tail)


def return_kernel(size, chunks, me_ref, source_ref, received_ref, *refs):
    outs, laid = refs[0:size], refs[size]
    lay_rows(chunks, 0, received_ref, None, laid)
    tok = outs[0].shape[0]
    together = PLACED // tok
    for shift in range(0, size, together):
        first = pl.multiple_of((me_ref[0] + shift) % size * tok, tok)
        found = find_rows(source_ref[:, pl.ds(first, PLACED)], laid)
        for n in range(together):
            outs[shift + n][...] = found[n * tok : (n + 1) * tok, :]


def return_rows(me, received, source_row, chunks, size):
    peers = received.shape[0]
    rows = source_row.shape[1]
    cols = chunks * HEAD
    tok = rows // size
    twice = jnp.concatenate([source_row, source_row], axis=1)
    return pl.pallas_call(
        functools.partial(return_kernel, size, chunks),
        grid_spec=pltpu.PrefetchScalarGridSpec(
            num_scalar_prefetch=1,
            grid=(1,),
            in_specs=[constant(twice.shape), constant(received.shape)],
            out_specs=[constant((tok, cols))] * size,
            scratch_shapes=[pltpu.VMEM((peers * SLOTS, cols), BF16)],
        ),
        out_shape=[jax.ShapeDtypeStruct((tok, cols), BF16)] * size,
        compiler_params=params(1),
        cost_estimate=cost(2 * rows * rows * cols, 4 * rows * cols),
        name="return_rows",
    )(me, twice, received)


def unpack_cotangent_kernel(
    first_tail, source_ref, x_ref, tail_ref, att_ref, inv_ref, gain_ref, out_ref, cross_ref, part_ref, laid
):
    @pl.when(pl.program_id(0) == 0)
    def _():
        lay_rows(out_ref.shape[1] // HEAD, first_tail, x_ref, tail_ref, laid)

    out_ref[...] = find_rows(source_ref[...], laid)
    cotangent_sums(att_ref, inv_ref, gain_ref, out_ref, cross_ref, part_ref)


def unpack_cotangent(received, tail, first_tail, source_row, att, inv_row, gain_row):
    rows, cols = att.shape
    lanes = pl.BlockSpec((1, PLACED), lambda i: (0, i))
    laid_rows = received.shape[0] * SLOTS + HEAD
    return pl.pallas_call(
        functools.partial(unpack_cotangent_kernel, first_tail),
        grid=(rows // PLACED,),
        in_specs=[
            lanes, whole(received.shape), whole(tail.shape), row_block(cols, PLACED), lanes, whole((1, cols)),
        ],
        out_specs=(row_block(cols, PLACED), lanes, whole((1, cols))),
        out_shape=(
            jax.ShapeDtypeStruct((rows, cols), BF16),
            jax.ShapeDtypeStruct((1, rows), F32),
            jax.ShapeDtypeStruct((1, cols), F32),
        ),
        scratch_shapes=[pltpu.VMEM((laid_rows, cols), BF16)],
        compiler_params=params(1),
        cost_estimate=cost(2 * rows * cols * laid_rows, 6 * rows * cols),
        name="unpack_cotangent",
    )(source_row, received, tail, att, inv_row, gain_row)


def merge_kernel(size, me_ref, via_ref, *refs):
    hops, grads, normed, outs = refs[0:size], refs[size : 2 * size], refs[2 * size : 3 * size], refs[3 * size :]
    shift = pl.program_id(0)
    via = as_column(via_ref[...].astype(F32)).astype(jnp.int32)
    peers = hops[0].shape[0] - TAIL
    pick = one_hot(iota((via.shape[0], peers), 1) == via)
    cols = grads[0].shape[1]
    for turn in range(size):

        @pl.when(shift == turn)
        def _():
            extra = dot(pick, hops[turn][0:peers, :])
            feat = extra.shape[1] - cols
            parts = hops[turn][peers:, :].astype(F32)
            outs[4][...] = parts[0:1, 0:feat] + parts[0:1, feat : 2 * feat]
            block = (grads[turn][...].astype(F32) + extra[:, 0:cols]).astype(BF16)
            outs[2][...] = block[:, 0:HEAD]
            outs[3][...] = block[:, HEAD : 2 * HEAD]
            outs[1][...] = block[:, 2 * HEAD :]
            outs[0][...] = (normed[turn][...].astype(F32) + extra[:, cols:]).astype(BF16)


def merge_rows(me, via_row, hops, grads, normed):
    size = len(grads)
    tok, cols = grads[0].shape
    feat = normed[0].shape[1]

    def column(width):
        return pl.BlockSpec((tok, width), lambda i, me_ref: (0, (me_ref[0] - i + size) % size))

    return pl.pallas_call(
        functools.partial(merge_kernel, size),
        grid_spec=pltpu.PrefetchScalarGridSpec(
            num_scalar_prefetch=1,
            grid=(size,),
            in_specs=[pl.BlockSpec((1, tok), lambda i, me_ref: (0, me_ref[0]))]
            + [constant(hops[0].shape)] * size
            + [constant((tok, cols))] * size
            + [constant((tok, feat))] * size,
            out_specs=[
                column(feat), column(feat), column(HEAD), column(HEAD),
                pl.BlockSpec((1, feat), lambda i, me_ref: (0, (me_ref[0] - i + size) % size)),
            ],
        ),
        out_shape=[
            jax.ShapeDtypeStruct((tok, size * width), BF16) for width in (feat, feat, HEAD, HEAD)
        ]
        + [jax.ShapeDtypeStruct((1, size * feat), F32)],
        compiler_params=params(1),
        cost_estimate=cost(2 * tok * SLOTS * size * (cols + feat), 4 * tok * size * (cols + feat)),
        name="merge_rows",
    )(me, via_row, *hops, *grads, *normed)


def rotated(x, size, first, sign):
    order = (first + sign * jnp.arange(size)) % size
    return x.reshape(size, -1)[order].reshape(1, -1)


def all_shifts(blocks, axis):
    return [lax.ppermute(b, axis, shifted(axis, n)) if n else b for n, b in enumerate(blocks)]


def cotangent_blocks(cotangent, me, feat):
    return all_shifts(
        [
            lax.dynamic_slice_in_dim(cotangent, (me + shift) % lax.axis_size("uly") * feat, feat, axis=1)
            for shift in range(lax.axis_size("uly"))
        ],
        "uly",
    )


def with_gain(hop, gain_total):
    high = lax.reduce_precision(gain_total, 8, 7)
    parts = jnp.concatenate([high, gain_total - high], axis=1).astype(BF16)
    parts = jnp.pad(parts, ((0, TAIL - 1), (0, hop.shape[1] - parts.shape[1])))
    return jnp.concatenate([hop, parts], axis=0)


def padded_path(me, kvq, cotangent, position, arrival_row, doc_row, gain_row):
    uly, ctx = lax.axis_size("uly"), lax.axis_size("ctx")
    tok, width = cotangent.shape
    rows, cols = tok * uly, kvq[0].shape[1]
    capacity = 2 * rows // ctx
    sent = ctx * capacity
    feat = width // uly
    position_in, position_out = rotated(position, uly, me, -1), rotated(position, uly, me, 1)
    kvq = spread_rows(jnp.concatenate(kvq, axis=0), position_in, sent)
    kvq = exchange(kvq.reshape(ctx, capacity, cols), "ctx").reshape(sent, cols)
    cot = jnp.concatenate(cotangent_blocks(cotangent, me, feat), axis=0)
    cot = spread_rows(cot, position_in, sent)
    cot = exchange(cot.reshape(ctx, capacity, feat), "ctx").reshape(sent, feat)
    kvq = take_rows(kvq, arrival_row)
    att, stats = forward_attention(kvq, doc_row)
    inv_root = lax.rsqrt(sum_over(stats[7:8, :], "uly") / width + 1e-06)
    normed = pack_normed(att, inv_root, gain_row, arrival_row, sent)
    normed = exchange(normed.reshape(ctx, capacity, feat), "ctx").reshape(sent, feat)
    cot, cross, gain_part = take_cotangent(cot, arrival_row, att, inv_root, gain_row)
    cross = sum_over(cross, "uly")
    grads = backward_attention(kvq, doc_row, att, cot, stats, inv_root, cross, gain_row)
    grads = spread_rows(grads, arrival_row, sent)
    grads, normed = lax.optimization_barrier((grads, normed))
    grads = exchange(grads.reshape(ctx, capacity, cols), "ctx").reshape(sent, cols)
    normed = all_shifts(jnp.split(take_rows(normed, position_out), uly), "uly")
    grads = all_shifts(jnp.split(take_rows(grads, position_out), uly), "uly")
    gain_total = sum_over(gain_part, "ctx")
    none = jnp.full((1, rows), -1, jnp.int32)
    hop = with_gain(jnp.zeros((ctx, cols + feat), BF16), gain_total)
    return merge_rows(me[None], none, all_shifts([hop] * uly, "uly"), grads, normed)


def passed_path(me, kvq, hop, cotangent, place, via, slot_source, ahead, back, doc_row, gain_row):
    uly, ctx = lax.axis_size("uly"), lax.axis_size("ctx")
    tok, width = cotangent.shape
    feat = width // uly
    wide, narrow = kvq[0].shape[1] // HEAD, feat // HEAD
    at = wide * SLOTS

    with jax.named_scope("rows_in"):
        tail = hop[:, 0:TAIL, :][ahead[0, 0:ctx]]
        kvq = exchange(pack_rows(me[None], kvq, place, ctx, tail), "ctx")
        tails = kvq[:, at:, :]

    with jax.named_scope("cotangent_in"):
        cot = pack_rows(me[None], cotangent_blocks(cotangent, me, feat), place, ctx)
        cot = exchange(cot, "ctx")

    with jax.named_scope("forward"):
        kvq = unpack_rows(kvq, slot_source, wide, tails)
        att, stats = forward_attention(kvq, doc_row)
        inv_root = lax.rsqrt(sum_over(stats[7:8, :], "uly") / width + 1e-06)

    with jax.named_scope("normed_out"):
        normed_sent, normed_slots = pack_normed_slots(att, inv_root, gain_row, slot_source, ctx)
        normed = exchange(normed_sent, "ctx")

    with jax.named_scope("backward"):
        cot, cross, gain_part = unpack_cotangent(
            cot, tails, wide, slot_source, att, inv_root, gain_row
        )
        cross = sum_over(cross, "uly")
        grads = backward_attention(kvq, doc_row, att, cot, stats, inv_root, cross, gain_row)

    with jax.named_scope("grads_out"):
        high = lax.reduce_precision(gain_part, 8, 7)
        part = jnp.concatenate([high, gain_part - high], axis=1).astype(BF16).reshape(-1, HEAD)
        part = jnp.pad(part, ((0, TAIL - part.shape[0]), (0, 0)))
        grads = pack_grads(grads, normed_slots, part, slot_source, ctx)
        grads, normed = lax.optimization_barrier((grads, normed))
        grads = exchange(grads, "ctx")

    with jax.named_scope("normed_rows"):
        normed = all_shifts(return_rows(me[None], normed, place, narrow, uly), "uly")
        grads, *normed = lax.optimization_barrier((grads, *normed))

    with jax.named_scope("passed_back"):
        hop = exchange(grads[:, at : at + TAIL, :][back[:, 0]], "ctx")

    with jax.named_scope("grad_rows"):
        rows_back = all_shifts(return_rows(me[None], grads, place, wide, uly), "uly")

    with jax.named_scope("gain_out"):
        parts = grads[:, at + TAIL : at + TAIL + 2 * narrow, :].astype(F32)
        gain_total = jnp.sum(parts[:, 0:narrow] + parts[:, narrow:], axis=0).reshape(1, feat)

    with jax.named_scope("merge"):
        hop = with_gain(hop.reshape(ctx, TAIL * HEAD), gain_total)
        return merge_rows(me[None], via, all_shifts([hop] * uly, "uly"), rows_back, normed)


def per_device(queries, keys, values, cotangent, norm_gain, owner_of_row, arrival, doc_start):
    tok, width = queries.shape
    uly, ctx = lax.axis_size("uly"), lax.axis_size("ctx")
    rows = tok * uly
    capacity = 2 * rows // ctx
    feat = width // uly
    me, here = lax.axis_index("uly"), lax.axis_index("ctx")

    with jax.named_scope("plan"):
        place, via, position, counts = plan_rows(owner_of_row[None, :], ctx, capacity)
        arrival_row = arrival[None, :]
        doc_row = doc_start[None, :]
        gain_row = lax.dynamic_slice_in_dim(norm_gain, me * feat, feat)[None, :]

    with jax.named_scope("rows_over_uly"):
        parts = split_rows(me[None], via, keys, values, queries, cotangent, uly, ctx)
        picked = all_shifts(parts[uly:], "uly")
        kvq = all_shifts(parts[0:uly], "uly")

    with jax.named_scope("first_hop"):
        hop = exchange(join_picked(counts, picked), "ctx")
        table = hop[:, TAIL, :]
        fits, slot_source, ahead, back = choose(here[None], table, arrival_row, capacity)

    outs = passed_path(
        me, kvq, hop, cotangent, place, via, slot_source, ahead, back, doc_row, gain_row
    )

    def keep(outs, cotangent, *kvq):
        return list(outs)

    def padded(outs, cotangent, *kvq):
        return list(padded_path(me, kvq, cotangent, position, arrival_row, doc_row, gain_row))

    outs = lax.cond(fits[0, 0] == 1, keep, padded, outs, cotangent, *kvq)
    return (*outs[0:4], outs[4].reshape(width))


def solution(mesh):
    split = P(("ctx", "uly"), None)
    plan = P("ctx")
    return jax.shard_map(
        per_device,
        mesh=mesh,
        in_specs=(split, split, split, split, P(), plan, plan, plan),
        out_specs=(split, split, split, split, P()),
        check_vma=False,
    )
```

```python
import functools
import math

import jax
import jax.numpy as jnp
from jax import lax
from jax.experimental import pallas as pl
from jax.experimental.pallas import tpu as pltpu
from jax.sharding import PartitionSpec as P

HEAD = 128
BLOCK = 256
DOC_MAX = 512
HIDDEN = -1e30
VMEM_BYTES = 26 * 1024 * 1024
F32 = jnp.float32
BF16 = jnp.bfloat16


def params(grid_axes):
    return pltpu.CompilerParams(
        dimension_semantics=("arbitrary",) * grid_axes, vmem_limit_bytes=VMEM_BYTES
    )


def whole(shape):
    return pl.BlockSpec(shape, lambda i: (0,) * len(shape))


def row_block(cols, rows=BLOCK):
    return pl.BlockSpec((rows, cols), lambda i: (i, 0))


def as_column(row):
    return jnp.transpose(jnp.broadcast_to(row, (8, row.shape[1])))[:, 0:1]


def dot(a, b):
    return lax.dot_general(a, b, (((1,), (0,)), ((), ())), preferred_element_type=F32)


def dot_nt(a, b):
    return lax.dot_general(a, b, (((1,), (1,)), ((), ())), preferred_element_type=F32)


def cost(flops, nbytes, exps=0):
    return pl.CostEstimate(flops=int(flops), bytes_accessed=int(nbytes), transcendentals=int(exps))


def spread_kernel(target_ref, x_ref, out_ref):
    first = pl.program_id(0) * BLOCK
    place = first + lax.broadcasted_iota(jnp.int32, (BLOCK, target_ref.shape[1]), 0)
    hit = (place == target_ref[...]).astype(F32).astype(BF16)
    out_ref[...] = dot(hit, x_ref[...]).astype(BF16)


def spread_rows(x, target_row, out_rows):
    rows, cols = x.shape
    return pl.pallas_call(
        spread_kernel,
        grid=(out_rows // BLOCK,),
        in_specs=[whole((1, rows)), whole((rows, cols))],
        out_specs=row_block(cols),
        out_shape=jax.ShapeDtypeStruct((out_rows, cols), BF16),
        compiler_params=params(1),
        cost_estimate=cost(2 * rows * cols * out_rows, 2 * cols * (rows + out_rows)),
        name="spread_rows",
    )(target_row, x)


def take_kernel(source_ref, x_ref, out_ref):
    source = as_column(source_ref[...].astype(F32)).astype(jnp.int32)
    lane = lax.broadcasted_iota(jnp.int32, (BLOCK, x_ref.shape[0]), 1)
    hit = (lane == source).astype(F32).astype(BF16)
    out_ref[...] = dot(hit, x_ref[...]).astype(BF16)


def take_rows(x, source_row):
    rows, cols = x.shape
    out_rows = source_row.shape[1]
    return pl.pallas_call(
        take_kernel,
        grid=(out_rows // BLOCK,),
        in_specs=[pl.BlockSpec((1, BLOCK), lambda i: (0, i)), whole((rows, cols))],
        out_specs=row_block(cols),
        out_shape=jax.ShapeDtypeStruct((out_rows, cols), BF16),
        compiler_params=params(1),
        cost_estimate=cost(2 * rows * cols * out_rows, 2 * cols * (rows + out_rows)),
        name="take_rows",
    )(source_row, x)


def key_window(block):
    start = max(0, block * BLOCK - DOC_MAX)
    return start, (block + 1) * BLOCK - start


def window_bias(doc_ref, block):
    start, size = key_window(block)
    key_pos = start + lax.broadcasted_iota(jnp.int32, (size, BLOCK), 0)
    query_pos = block * BLOCK + lax.broadcasted_iota(jnp.int32, (size, BLOCK), 1)
    first_key = doc_ref[0:1, block * BLOCK : (block + 1) * BLOCK]
    return jnp.where((key_pos >= first_key) & (key_pos <= query_pos), 0.0, HIDDEN)


LOG2E = math.log2(math.e)


def forward_kernel(heads, doc_ref, kvq_ref, att_ref, stat_ref, value_t, bias_ref):
    rows = kvq_ref.shape[0]
    scale = HEAD ** (-0.5) * LOG2E
    value_t[...] = jnp.transpose(kvq_ref[:, HEAD : 2 * HEAD].astype(F32)).astype(BF16)
    for block in range(rows // BLOCK):
        start, size = key_window(block)
        q_rows = slice(block * BLOCK, (block + 1) * BLOCK)
        bias_ref[0:size, :] = window_bias(doc_ref, block)
        squares = jnp.zeros((1, BLOCK), F32)
        for head in range(heads):
            lanes = slice(head * HEAD, (head + 1) * HEAD)
            query = kvq_ref[q_rows, (head + 2) * HEAD : (head + 3) * HEAD]
            scores = dot_nt(kvq_ref[start : start + size, 0:HEAD], query) * scale + bias_ref[0:size, :]
            peak = jnp.max(scores, axis=0, keepdims=True)
            raised = jnp.exp2(scores - peak)
            total = jnp.sum(raised, axis=0, keepdims=True)
            weights = (raised * (1.0 / total)).astype(BF16)
            out_t = dot(value_t[:, start : start + size], weights)
            out = out_t.astype(BF16).astype(F32)
            squares = squares + jnp.sum(out * out, axis=0, keepdims=True)
            att_ref[q_rows, lanes] = jnp.transpose(out).astype(BF16)
            stat_ref[head : head + 1, q_rows] = peak + jnp.log2(total)
        stat_ref[7:8, q_rows] = squares


def forward_attention(kvq, doc_row):
    rows, cols = kvq.shape
    heads = cols // HEAD - 2
    pairs = rows * 576 * heads
    return pl.pallas_call(
        functools.partial(forward_kernel, heads),
        out_shape=(
            jax.ShapeDtypeStruct((rows, heads * HEAD), BF16),
            jax.ShapeDtypeStruct((8, rows), F32),
        ),
        scratch_shapes=[pltpu.VMEM((HEAD, rows), BF16), pltpu.VMEM((3 * BLOCK, BLOCK), F32)],
        compiler_params=pltpu.CompilerParams(vmem_limit_bytes=VMEM_BYTES),
        cost_estimate=cost(pairs * 16 * HEAD, 4 * rows * cols, pairs),
        name="forward_attention",
    )(doc_row, kvq)


def pack_normed_kernel(target_ref, att_ref, inv_ref, gain_ref, out_ref, normed):
    @pl.when(pl.program_id(0) == 0)
    def _():
        inv = as_column(inv_ref[...])
        normed[...] = (gain_ref[...] * att_ref[...].astype(F32) * inv).astype(BF16)

    spread_kernel(target_ref, normed, out_ref)


def pack_normed(att, inv_row, gain_row, target_row, out_rows):
    rows, cols = att.shape
    return pl.pallas_call(
        pack_normed_kernel,
        grid=(out_rows // BLOCK,),
        in_specs=[whole((1, rows)), whole((rows, cols)), whole((1, rows)), whole((1, cols))],
        out_specs=row_block(cols),
        out_shape=jax.ShapeDtypeStruct((out_rows, cols), BF16),
        scratch_shapes=[pltpu.VMEM((rows, cols), BF16)],
        compiler_params=params(1),
        cost_estimate=cost(2 * rows * cols * out_rows, 2 * cols * (rows + out_rows)),
        name="pack_normed",
    )(target_row, att, inv_row, gain_row)


def take_cotangent_kernel(source_ref, x_ref, att_ref, inv_ref, gain_ref, out_ref, cross_ref, part_ref):
    take_kernel(source_ref, x_ref, out_ref)
    cotangent_sums(att_ref, inv_ref, gain_ref, out_ref, cross_ref, part_ref)


def cotangent_sums(att_ref, inv_ref, gain_ref, out_ref, cross_ref, part_ref):
    product = out_ref[...].astype(F32) * att_ref[...].astype(F32)
    cross = jnp.sum(product * gain_ref[...], axis=1, keepdims=True)
    cross_ref[...] = jnp.transpose(jnp.broadcast_to(cross, (cross.shape[0], HEAD)))[0:1, :]

    @pl.when(pl.program_id(0) == 0)
    def _():
        part_ref[...] = jnp.zeros_like(part_ref)

    part_ref[...] += jnp.sum(product * as_column(inv_ref[...]), axis=0, keepdims=True)


def take_cotangent(received, source_row, att, inv_row, gain_row):
    rows, cols = att.shape
    lanes = pl.BlockSpec((1, BLOCK), lambda i: (0, i))
    return pl.pallas_call(
        take_cotangent_kernel,
        grid=(rows // BLOCK,),
        in_specs=[lanes, whole(received.shape), row_block(cols), lanes, whole((1, cols))],
        out_specs=(row_block(cols), lanes, whole((1, cols))),
        out_shape=(
            jax.ShapeDtypeStruct((rows, cols), BF16),
            jax.ShapeDtypeStruct((1, rows), F32),
            jax.ShapeDtypeStruct((1, cols), F32),
        ),
        compiler_params=params(1),
        cost_estimate=cost(2 * rows * cols * received.shape[0], 2 * cols * (3 * rows)),
        name="take_cotangent",
    )(source_row, received, att, inv_row, gain_row)


def backward_kernel(
    heads, doc_ref, kvq_ref, att_ref, cot_ref, stat_ref, inv_ref, cross_ref, gain_ref,
    out_ref, key_t, key_sum, value_sum, bias_ref,
):
    rows = kvq_ref.shape[0]
    width = heads * HEAD * 8
    scale = HEAD ** (-0.5)
    key_t[...] = jnp.transpose(kvq_ref[:, 0:HEAD].astype(F32)).astype(BF16)
    key_sum[...] = jnp.zeros_like(key_sum)
    value_sum[...] = jnp.zeros_like(value_sum)
    for block in range(rows // BLOCK):
        start, size = key_window(block)
        q_rows = slice(block * BLOCK, (block + 1) * BLOCK)
        keys = slice(start, start + size)
        bias_ref[0:size, :] = window_bias(doc_ref, block)
        inv = as_column(inv_ref[:, q_rows])
        shift = as_column(cross_ref[:, q_rows]) * (inv * inv * inv * (1.0 / width))
        for head in range(heads):
            lanes = slice(head * HEAD, (head + 1) * HEAD)
            wide = slice((head + 2) * HEAD, (head + 3) * HEAD)
            query = kvq_ref[q_rows, wide]
            grad = (
                gain_ref[:, lanes] * cot_ref[q_rows, lanes].astype(F32) * inv
                - att_ref[q_rows, lanes].astype(F32) * shift
            ).astype(BF16)
            scores = dot_nt(kvq_ref[keys, 0:HEAD], query) * (scale * LOG2E) + bias_ref[0:size, :]
            weights = jnp.exp2(scores - stat_ref[head : head + 1, q_rows])
            grad_weights = dot_nt(kvq_ref[keys, HEAD : 2 * HEAD], grad)
            centre = jnp.sum(weights * grad_weights, axis=0, keepdims=True)
            grad_scores = (weights * (grad_weights - centre)).astype(BF16)
            key_sum[keys, :] += dot(grad_scores, query)
            value_sum[keys, :] += dot(weights.astype(BF16), grad)
            grad_query = dot(key_t[:, keys], grad_scores) * scale
            out_ref[q_rows, wide] = jnp.transpose(grad_query).astype(BF16)
    out_ref[:, 0:HEAD] = (key_sum[...] * scale).astype(BF16)
    out_ref[:, HEAD : 2 * HEAD] = value_sum[...].astype(BF16)


def backward_attention(kvq, doc_row, att, cot, stats, inv_row, cross_row, gain_row):
    rows, cols = kvq.shape
    heads = cols // HEAD - 2
    pairs = rows * 576 * heads
    return pl.pallas_call(
        functools.partial(backward_kernel, heads),
        out_shape=jax.ShapeDtypeStruct((rows, cols), BF16),
        scratch_shapes=[
            pltpu.VMEM((HEAD, rows), BF16),
            pltpu.VMEM((rows, HEAD), F32),
            pltpu.VMEM((rows, HEAD), F32),
            pltpu.VMEM((3 * BLOCK, BLOCK), F32),
        ],
        compiler_params=pltpu.CompilerParams(vmem_limit_bytes=VMEM_BYTES),
        cost_estimate=cost(pairs * 30 * HEAD, 8 * rows * cols, pairs),
        name="backward_attention",
    )(doc_row, kvq, att, cot, stats, inv_row, cross_row, gain_row)


def sum_over(x, axis, rounds):
    size = lax.axis_size(axis)
    for steps in rounds:
        x = sum([lax.ppermute(x, axis, [(i, i ^ step) for i in range(size)]) for step in steps], x)
    return x


ULY_ROUNDS = ((1,), (2, 4, 6))
CTX_ROUNDS = ((1,), (2,), (4,), (8,), (16,))


def shifted(axis, by):
    size = lax.axis_size(axis)
    return [(i, (i + by) % size) for i in range(size)]


def exchange(x, axis):
    return lax.all_to_all(x, axis, split_axis=0, concat_axis=0, tiled=True)


SLOTS = 32
TAIL = 16


def tile(n):
    return slice(n * HEAD, (n + 1) * HEAD)


PLACED = 512


def one_hot(flags):
    return flags.astype(F32).astype(BF16)


def iota(shape, dim):
    return lax.broadcasted_iota(jnp.int32, shape, dim)


def constant(shape):
    return pl.BlockSpec(shape, lambda i, *_: (0,) * len(shape))


def cube(count, chunk_rows):
    return pl.BlockSpec((count, chunk_rows, HEAD), lambda i, *_: (i, 0, 0))


def spread_body(x_ref, target_ref, out_ref, chunks):
    place = pl.program_id(0) * PLACED + iota((PLACED, target_ref.shape[1]), 0)
    found = dot(one_hot(place == target_ref[...]), x_ref[...]).astype(BF16)
    for n in range(chunks):
        out_ref[:, n * SLOTS : (n + 1) * SLOTS, :] = found[:, tile(n)].reshape(-1, SLOTS, HEAD)


def plan_kernel(ctx, capacity, owner_ref, place_ref, via_ref, position_ref, count_ref):
    owner = owner_ref[...]
    rows = owner.shape[1]
    mine = iota((ctx, rows), 0) == owner
    mine_wide = mine.astype(F32)
    earlier = one_hot(iota((rows, rows), 0) < iota((rows, rows), 1))
    rank = jnp.sum(dot(mine_wide.astype(BF16), earlier) * mine_wide, axis=0, keepdims=True)
    counts = jnp.sum(mine_wide, axis=1, keepdims=True)
    beyond = jnp.broadcast_to(jnp.maximum(counts - SLOTS, 0.0), (ctx, HEAD))
    lower = one_hot(iota((ctx, ctx), 1) < iota((ctx, ctx), 0))
    begin = dot(lower, beyond.astype(BF16))[:, 0:1]
    via = jnp.sum(begin * mine_wide, axis=0, keepdims=True) + rank - SLOTS
    rank = rank.astype(jnp.int32)
    inside = rank < SLOTS
    place_ref[...] = jnp.where(inside, owner * SLOTS + rank, -1)
    via_ref[...] = jnp.where(inside, -1, via.astype(jnp.int32))
    position_ref[...] = owner * capacity + rank
    padded = jnp.concatenate([jnp.broadcast_to(counts, (ctx, HEAD)), jnp.zeros((HEAD - ctx, HEAD), F32)], axis=0)
    count_ref[...] = jnp.transpose(padded)[0:TAIL, :].astype(BF16)


def plan_rows(owner_row, ctx, capacity):
    rows = owner_row.shape[1]
    line = jax.ShapeDtypeStruct((1, rows), jnp.int32)
    return pl.pallas_call(
        functools.partial(plan_kernel, ctx, capacity),
        out_shape=(line, line, line, jax.ShapeDtypeStruct((TAIL, HEAD), BF16)),
        compiler_params=pltpu.CompilerParams(vmem_limit_bytes=VMEM_BYTES),
        cost_estimate=cost(2 * rows * rows * ctx, 8 * rows),
        name="plan_rows",
    )(owner_row)


def choice_kernel(
    capacity, here_ref, table_ref, arrival_ref, fits_ref, source_ref, ahead_ref, back_ref
):
    ctx = table_ref.shape[0]
    here = here_ref[0]
    beyond = jnp.maximum(table_ref[:, 0:HEAD].astype(F32) - SLOTS, 0.0)
    before = one_hot(iota((HEAD, HEAD), 0) < iota((HEAD, HEAD), 1))
    begin = dot(beyond.astype(BF16), before)
    end = begin + beyond
    most = jnp.max(jnp.sum(beyond, axis=1, keepdims=True), axis=0, keepdims=True)
    worst = jnp.zeros((1, HEAD), F32)
    for n in range(ctx):
        led = ((begin <= n) & (n < end)).astype(F32)
        worst = jnp.maximum(worst, jnp.sum(led, axis=0, keepdims=True))
    worst = jnp.max(worst, axis=1, keepdims=True)
    fits = (most <= ctx) & (worst <= 1.0)
    fits_ref[...] = jnp.broadcast_to(fits.astype(jnp.int32), fits_ref.shape)
    number = here.astype(F32)
    led = ((begin <= number) & (number < end)).astype(F32)
    group = iota((ctx, HEAD), 0).astype(F32)
    lane = iota((ctx, HEAD), 1)
    ahead = jnp.minimum(jnp.sum(led * group, axis=0, keepdims=True), ctx - 1.0)
    ahead_ref[...] = ahead.astype(jnp.int32)
    back = jnp.minimum(jnp.sum(led * lane.astype(F32), axis=1, keepdims=True), ctx - 1.0)
    back_ref[...] = jnp.broadcast_to(back, (ctx, HEAD)).astype(jnp.int32)
    begin_here = jnp.sum(jnp.where(lane == here, begin, 0.0), axis=1, keepdims=True)
    arrival = arrival_ref[...]
    rows = arrival.shape[1]
    source_group = arrival // capacity
    rank = arrival - source_group * capacity
    passed = jnp.sum(
        jnp.where(iota((ctx, rows), 0) == source_group, begin_here, 0.0), axis=0, keepdims=True
    ).astype(jnp.int32)
    source_ref[...] = jnp.where(
        rank < SLOTS, source_group * SLOTS + rank, ctx * SLOTS + passed + rank - SLOTS
    )


def choose(here, table, arrival_row, capacity):
    ctx = table.shape[0]
    return pl.pallas_call(
        functools.partial(choice_kernel, capacity),
        grid_spec=pltpu.PrefetchScalarGridSpec(
            num_scalar_prefetch=1,
            grid=(1,),
            in_specs=[constant(table.shape), constant(arrival_row.shape)],
            out_specs=[
                constant((8, HEAD)), constant(arrival_row.shape), constant((1, HEAD)), constant((ctx, HEAD)),
            ],
        ),
        out_shape=[
            jax.ShapeDtypeStruct((8, HEAD), jnp.int32),
            jax.ShapeDtypeStruct(arrival_row.shape, jnp.int32),
            jax.ShapeDtypeStruct((1, HEAD), jnp.int32),
            jax.ShapeDtypeStruct((ctx, HEAD), jnp.int32),
        ],
        compiler_params=params(1),
        cost_estimate=cost(1e6, 1e5),
        name="choose",
    )(here, table, arrival_row)


def pick_kernel(size, me_ref, via_ref, cot_ref, *picked):
    peers = picked[0].shape[0]
    pick = one_hot(iota((peers, via_ref.shape[1]), 0) == via_ref[...])
    for turn in range(size):

        @pl.when(pl.program_id(0) == turn)
        def _():
            picked[turn][...] = dot(pick, cot_ref[...]).astype(BF16)


def pick_rows(me, via_row, cotangent, size, peers):
    tok, width = cotangent.shape
    feat = width // size
    return pl.pallas_call(
        functools.partial(pick_kernel, size),
        grid_spec=pltpu.PrefetchScalarGridSpec(
            num_scalar_prefetch=1,
            grid=(size,),
            in_specs=[
                pl.BlockSpec((1, tok), lambda i, me_ref: (0, me_ref[0])),
                pl.BlockSpec((tok, feat), lambda i, me_ref: (0, (me_ref[0] + i) % size)),
            ],
            out_specs=[constant((peers, feat))] * size,
        ),
        out_shape=[jax.ShapeDtypeStruct((peers, feat), BF16)] * size,
        compiler_params=params(1),
        cost_estimate=cost(2 * peers * tok * width, 2 * tok * width),
        name="pick_rows",
    )(me, via_row, cotangent)


def chunked(pieces):
    rows = pieces[0].shape[0]
    copies = one_hot(iota((rows * TAIL, rows), 0) // TAIL == iota((rows * TAIL, rows), 1))
    turn = iota((rows * TAIL, HEAD), 0) % TAIL
    chunks = jnp.zeros((rows * TAIL, HEAD), F32)
    n = 0
    for piece in pieces:
        found = dot(copies, piece)
        for at in range(piece.shape[1] // HEAD):
            chunks = jnp.where(turn == n, found[:, tile(at)], chunks)
            n += 1
    return chunks.astype(BF16).reshape(rows, TAIL, HEAD)


def join_kernel(count_ref, via_ref, kvq_ref, *refs):
    *picked, out_ref = refs
    total = picked[0][...].astype(F32)
    for ref in picked[1:]:
        total = total + ref[...].astype(F32)
    peers = total.shape[0]
    hit = one_hot(iota((peers, via_ref.shape[1]), 0) == via_ref[...])
    rows = dot(hit, kvq_ref[...]).astype(BF16)
    out_ref[:, 0:TAIL, :] = chunked((rows, total.astype(BF16)))
    out_ref[:, TAIL:, :] = jnp.broadcast_to(count_ref[...][None], (peers, TAIL, HEAD))


def join_picked(counts, via_row, kvq, picked):
    peers = picked[0].shape[0]
    return pl.pallas_call(
        join_kernel,
        out_shape=jax.ShapeDtypeStruct((peers, 2 * TAIL, HEAD), BF16),
        compiler_params=pltpu.CompilerParams(vmem_limit_bytes=VMEM_BYTES),
        cost_estimate=cost(1e8, 4e6),
        name="join_picked",
    )(counts, via_row, kvq, *picked)


def tail_kernel(ahead_ref, hop_ref, packed_ref, out_ref):
    for peer in range(out_ref.shape[0]):
        out_ref[peer] = hop_ref[ahead_ref[peer]]


def add_tail(ahead, hop, packed):
    peers, depth, _ = packed.shape
    block = (peers, TAIL, HEAD)
    return pl.pallas_call(
        tail_kernel,
        grid_spec=pltpu.PrefetchScalarGridSpec(
            num_scalar_prefetch=1,
            grid=(1,),
            in_specs=[
                pl.BlockSpec(block, lambda i, *_: (0, 0, 0)),
                pl.BlockSpec(memory_space=pl.ANY),
            ],
            out_specs=pl.BlockSpec(block, lambda i, *_: (0, depth // TAIL - 1, 0)),
        ),
        out_shape=jax.ShapeDtypeStruct(packed.shape, BF16),
        input_output_aliases={2: 0},
        compiler_params=params(1),
        cost_estimate=cost(1e5, 1e6),
        name="add_tail",
    )(ahead, hop, packed)


def pack_kernel(size, chunks, me_ref, target_ref, *refs):
    blocks, out_ref, rows = refs[0:size], refs[size], refs[size + 1]

    @pl.when(pl.program_id(0) == 0)
    def _():
        tok = blocks[0].shape[0]
        for shift in range(size):
            first = pl.multiple_of((me_ref[0] + size - shift) % size * tok, tok)
            rows[pl.ds(first, tok), :] = blocks[shift][...]

    spread_body(rows, target_ref, out_ref, chunks)


def pack_rows(me, blocks, target_row, peers, room=0):
    size = len(blocks)
    tok, cols = blocks[0].shape
    rows = tok * size
    chunks = cols // HEAD
    step = PLACED // SLOTS
    depth = chunks * SLOTS + room
    return pl.pallas_call(
        functools.partial(pack_kernel, size, chunks),
        grid_spec=pltpu.PrefetchScalarGridSpec(
            num_scalar_prefetch=1,
            grid=(peers // step,),
            in_specs=[constant((1, rows))] + [constant((tok, cols))] * size,
            out_specs=cube(step, depth),
            scratch_shapes=[pltpu.VMEM((rows, cols), BF16)],
        ),
        out_shape=jax.ShapeDtypeStruct((peers, depth, HEAD), BF16),
        compiler_params=params(1),
        cost_estimate=cost(2 * rows * cols * peers * SLOTS, 4 * rows * cols),
        name="pack_rows",
    )(me, target_row, *blocks)


def pack_normed_slots_kernel(chunks, target_ref, att_ref, inv_ref, gain_ref, out_ref, normed_ref):
    @pl.when(pl.program_id(0) == 0)
    def _():
        inv = as_column(inv_ref[...])
        normed_ref[...] = (gain_ref[...] * att_ref[...].astype(F32) * inv).astype(BF16)

    spread_body(normed_ref, target_ref, out_ref, chunks)


def pack_normed_slots(att, inv_row, gain_row, target_row, peers):
    rows, cols = att.shape
    chunks = cols // HEAD
    step = PLACED // SLOTS
    return pl.pallas_call(
        functools.partial(pack_normed_slots_kernel, chunks),
        grid=(peers // step,),
        in_specs=[whole((1, rows)), whole((rows, cols)), whole((1, rows)), whole((1, cols))],
        out_specs=(cube(step, chunks * SLOTS), whole((rows, cols))),
        out_shape=(
            jax.ShapeDtypeStruct((peers, chunks * SLOTS, HEAD), BF16),
            jax.ShapeDtypeStruct((rows, cols), BF16),
        ),
        compiler_params=params(1),
        cost_estimate=cost(2 * rows * cols * peers * SLOTS, 6 * rows * cols),
        name="pack_normed_slots",
    )(target_row, att, inv_row, gain_row)


def pack_grads_kernel(target_ref, grads_ref, normed_ref, part_ref, out_ref):
    chunks = grads_ref.shape[1] // HEAD
    step = out_ref.shape[0]
    peers = pl.num_programs(0) * step
    row = iota((PLACED + step, target_ref.shape[1]), 0)
    main = pl.program_id(0) * PLACED + row
    passed = peers * SLOTS + pl.program_id(0) * step + row - PLACED
    hit = one_hot(jnp.where(row < PLACED, main, passed) == target_ref[...])
    found = dot(hit, grads_ref[...]).astype(BF16)
    for n in range(chunks):
        out_ref[:, n * SLOTS : (n + 1) * SLOTS, :] = found[0:PLACED, tile(n)].reshape(-1, SLOTS, HEAD)
    normed = dot(hit[PLACED:, :], normed_ref[...]).astype(BF16)
    at = chunks * SLOTS
    out_ref[:, at : at + TAIL, :] = chunked((found[PLACED:, :], normed))
    out_ref[:, at + TAIL :, :] = jnp.broadcast_to(part_ref[...][None], (step, TAIL, HEAD))


def pack_grads(grads, normed, part, target_row, peers):
    rows, cols = grads.shape
    step = PLACED // SLOTS
    depth = cols // HEAD * SLOTS + 2 * TAIL
    return pl.pallas_call(
        pack_grads_kernel,
        grid=(peers // step,),
        in_specs=[whole((1, rows)), whole(grads.shape), whole(normed.shape), whole(part.shape)],
        out_specs=cube(step, depth),
        out_shape=jax.ShapeDtypeStruct((peers, depth, HEAD), BF16),
        compiler_params=params(1),
        cost_estimate=cost(4 * rows * cols * peers * SLOTS, 6 * rows * cols),
        name="pack_grads",
    )(target_row, grads, normed, part)


def lay_rows(chunks, received_ref, laid):
    main = received_ref.shape[0] * SLOTS
    for n in range(chunks):
        laid[0:main, tile(n)] = received_ref[:, n * SLOTS : (n + 1) * SLOTS, :].reshape(main, HEAD)


def find_rows(source, laid):
    source = as_column(source.astype(F32)).astype(jnp.int32)
    lane = iota((source.shape[0], laid.shape[0]), 1)
    return dot(one_hot(lane == source), laid[...]).astype(BF16)


def unpack_kernel(chunks, source_ref, received_ref, out_ref, more_ref, laid):
    @pl.when(pl.program_id(0) == 0)
    def _():
        lay_rows(chunks, received_ref, laid)
        peers = received_ref.shape[0]
        main = peers * SLOTS
        laid[main:, :] = jnp.zeros_like(laid[main:, :])
        more_ref[...] = jnp.zeros_like(more_ref)
        tails = received_ref[:, chunks * SLOTS :, :].reshape(peers * TAIL, HEAD)
        lane = iota((peers, peers * TAIL), 1) - iota((peers, peers * TAIL), 0) * TAIL
        for n in range(TAIL):
            rows = dot(one_hot(lane == n), tails).astype(BF16)
            if n < chunks:
                laid[main : main + peers, tile(n)] = rows
            else:
                more_ref[0:peers, tile(n - chunks)] = rows

    out_ref[...] = find_rows(source_ref[...], laid)


def unpack_rows(received, source_row, chunks):
    peers = received.shape[0]
    rows = source_row.shape[1]
    cols = chunks * HEAD
    more = (HEAD, (TAIL - chunks) * HEAD)
    laid_rows = peers * SLOTS + HEAD
    return pl.pallas_call(
        functools.partial(unpack_kernel, chunks),
        grid=(rows // PLACED,),
        in_specs=[pl.BlockSpec((1, PLACED), lambda i: (0, i)), whole(received.shape)],
        out_specs=(row_block(cols, PLACED), whole(more)),
        out_shape=(
            jax.ShapeDtypeStruct((rows, cols), BF16),
            jax.ShapeDtypeStruct(more, BF16),
        ),
        scratch_shapes=[pltpu.VMEM((laid_rows, cols), BF16)],
        compiler_params=params(1),
        cost_estimate=cost(2 * rows * cols * laid_rows, 4 * rows * cols),
        name="unpack_rows",
    )(source_row, received)


def return_kernel(size, chunks, me_ref, source_ref, received_ref, *refs):
    outs, laid = refs[0:size], refs[size]
    lay_rows(chunks, received_ref, laid)
    tok = outs[0].shape[0]
    together = PLACED // tok
    for shift in range(0, size, together):
        first = pl.multiple_of((me_ref[0] + shift) % size * tok, tok)
        found = find_rows(source_ref[:, pl.ds(first, PLACED)], laid)
        for n in range(together):
            outs[shift + n][...] = found[n * tok : (n + 1) * tok, :]


def return_rows(me, received, source_row, chunks, size):
    peers = received.shape[0]
    rows = source_row.shape[1]
    cols = chunks * HEAD
    tok = rows // size
    twice = jnp.concatenate([source_row, source_row], axis=1)
    return pl.pallas_call(
        functools.partial(return_kernel, size, chunks),
        grid_spec=pltpu.PrefetchScalarGridSpec(
            num_scalar_prefetch=1,
            grid=(1,),
            in_specs=[constant(twice.shape), constant(received.shape)],
            out_specs=[constant((tok, cols))] * size,
            scratch_shapes=[pltpu.VMEM((peers * SLOTS, cols), BF16)],
        ),
        out_shape=[jax.ShapeDtypeStruct((tok, cols), BF16)] * size,
        compiler_params=params(1),
        cost_estimate=cost(2 * rows * rows * cols, 4 * rows * cols),
        name="return_rows",
    )(me, twice, received)


def unpack_cotangent_kernel(
    source_ref, x_ref, more_ref, att_ref, inv_ref, gain_ref, out_ref, cross_ref, part_ref, laid
):
    @pl.when(pl.program_id(0) == 0)
    def _():
        lay_rows(out_ref.shape[1] // HEAD, x_ref, laid)
        laid[x_ref.shape[0] * SLOTS :, :] = more_ref[...]

    out_ref[...] = find_rows(source_ref[...], laid)
    cotangent_sums(att_ref, inv_ref, gain_ref, out_ref, cross_ref, part_ref)


def unpack_cotangent(received, more, source_row, att, inv_row, gain_row):
    rows, cols = att.shape
    lanes = pl.BlockSpec((1, PLACED), lambda i: (0, i))
    laid_rows = received.shape[0] * SLOTS + HEAD
    return pl.pallas_call(
        unpack_cotangent_kernel,
        grid=(rows // PLACED,),
        in_specs=[
            lanes, whole(received.shape), whole(more.shape), row_block(cols, PLACED), lanes, whole((1, cols)),
        ],
        out_specs=(row_block(cols, PLACED), lanes, whole((1, cols))),
        out_shape=(
            jax.ShapeDtypeStruct((rows, cols), BF16),
            jax.ShapeDtypeStruct((1, rows), F32),
            jax.ShapeDtypeStruct((1, cols), F32),
        ),
        scratch_shapes=[pltpu.VMEM((laid_rows, cols), BF16)],
        compiler_params=params(1),
        cost_estimate=cost(2 * rows * cols * laid_rows, 6 * rows * cols),
        name="unpack_cotangent",
    )(source_row, received, more, att, inv_row, gain_row)


def merge_kernel(size, me_ref, via_ref, *refs):
    hops, grads, normed, outs = refs[0:size], refs[size : 2 * size], refs[2 * size : 3 * size], refs[3 * size :]
    shift = pl.program_id(0)
    via = as_column(via_ref[...].astype(F32)).astype(jnp.int32)
    peers = hops[0].shape[0] - TAIL
    pick = one_hot(iota((via.shape[0], peers), 1) == via)
    cols = grads[0].shape[1]
    for turn in range(size):

        @pl.when(shift == turn)
        def _():
            extra = dot(pick, hops[turn][0:peers, :])
            feat = extra.shape[1] - cols
            parts = hops[turn][peers:, :].astype(F32)
            outs[4][...] = parts[0:1, 0:feat] + parts[0:1, feat : 2 * feat]
            block = (grads[turn][...].astype(F32) + extra[:, 0:cols]).astype(BF16)
            outs[2][...] = block[:, 0:HEAD]
            outs[3][...] = block[:, HEAD : 2 * HEAD]
            outs[1][...] = block[:, 2 * HEAD :]
            outs[0][...] = (normed[turn][...].astype(F32) + extra[:, cols:]).astype(BF16)


def merge_rows(me, via_row, hops, grads, normed):
    size = len(grads)
    tok, cols = grads[0].shape
    feat = normed[0].shape[1]

    def column(width):
        return pl.BlockSpec((tok, width), lambda i, me_ref: (0, (me_ref[0] - i + size) % size))

    return pl.pallas_call(
        functools.partial(merge_kernel, size),
        grid_spec=pltpu.PrefetchScalarGridSpec(
            num_scalar_prefetch=1,
            grid=(size,),
            in_specs=[pl.BlockSpec((1, tok), lambda i, me_ref: (0, me_ref[0]))]
            + [constant(hops[0].shape)] * size
            + [constant((tok, cols))] * size
            + [constant((tok, feat))] * size,
            out_specs=[
                column(feat), column(feat), column(HEAD), column(HEAD),
                pl.BlockSpec((1, feat), lambda i, me_ref: (0, (me_ref[0] - i + size) % size)),
            ],
        ),
        out_shape=[
            jax.ShapeDtypeStruct((tok, size * width), BF16) for width in (feat, feat, HEAD, HEAD)
        ]
        + [jax.ShapeDtypeStruct((1, size * feat), F32)],
        compiler_params=params(1),
        cost_estimate=cost(2 * tok * SLOTS * size * (cols + feat), 4 * tok * size * (cols + feat)),
        name="merge_rows",
    )(me, via_row, *hops, *grads, *normed)


def rotated(x, size, first, sign):
    order = (first + sign * jnp.arange(size)) % size
    return x.reshape(size, -1)[order].reshape(1, -1)


def all_shifts(blocks, axis):
    return [lax.ppermute(b, axis, shifted(axis, n)) if n else b for n, b in enumerate(blocks)]


def cotangent_blocks(cotangent, me, feat):
    return all_shifts(
        [
            lax.dynamic_slice_in_dim(cotangent, (me + shift) % lax.axis_size("uly") * feat, feat, axis=1)
            for shift in range(lax.axis_size("uly"))
        ],
        "uly",
    )


def with_gain(hop, gain_total):
    high = lax.reduce_precision(gain_total, 8, 7)
    parts = jnp.concatenate([high, gain_total - high], axis=1).astype(BF16)
    parts = jnp.pad(parts, ((0, TAIL - 1), (0, hop.shape[1] - parts.shape[1])))
    return jnp.concatenate([hop, parts], axis=0)


def padded_path(me, kvq, cotangent, position, arrival_row, doc_row, gain_row):
    uly, ctx = lax.axis_size("uly"), lax.axis_size("ctx")
    tok, width = cotangent.shape
    rows, cols = kvq.shape
    capacity = 2 * rows // ctx
    sent = ctx * capacity
    feat = width // uly
    position_in, position_out = rotated(position, uly, me, -1), rotated(position, uly, me, 1)
    kvq = spread_rows(kvq, position, sent)
    kvq = exchange(kvq.reshape(ctx, capacity, cols), "ctx").reshape(sent, cols)
    cot = jnp.concatenate(cotangent_blocks(cotangent, me, feat), axis=0)
    cot = spread_rows(cot, position_in, sent)
    cot = exchange(cot.reshape(ctx, capacity, feat), "ctx").reshape(sent, feat)
    kvq = take_rows(kvq, arrival_row)
    att, stats = forward_attention(kvq, doc_row)
    inv_root = lax.rsqrt(sum_over(stats[7:8, :], "uly", ULY_ROUNDS) / width + 1e-06)
    normed = pack_normed(att, inv_root, gain_row, arrival_row, sent)
    normed = exchange(normed.reshape(ctx, capacity, feat), "ctx").reshape(sent, feat)
    cot, cross, gain_part = take_cotangent(cot, arrival_row, att, inv_root, gain_row)
    cross = sum_over(cross, "uly", ULY_ROUNDS)
    grads = backward_attention(kvq, doc_row, att, cot, stats, inv_root, cross, gain_row)
    grads = spread_rows(grads, arrival_row, sent)
    grads, normed = lax.optimization_barrier((grads, normed))
    grads = exchange(grads.reshape(ctx, capacity, cols), "ctx").reshape(sent, cols)
    normed = all_shifts(jnp.split(take_rows(normed, position_out), uly), "uly")
    grads = all_shifts(jnp.split(take_rows(grads, position_out), uly), "uly")
    gain_total = sum_over(gain_part, "ctx", CTX_ROUNDS)
    none = jnp.full((1, rows), -1, jnp.int32)
    hop = with_gain(jnp.zeros((ctx, cols + feat), BF16), gain_total)
    return merge_rows(me[None], none, all_shifts([hop] * uly, "uly"), grads, normed)


def passed_path(me, kvq, hop, cotangent, place, via, slot_source, ahead, back, doc_row, gain_row):
    uly, ctx = lax.axis_size("uly"), lax.axis_size("ctx")
    tok, width = cotangent.shape
    feat = width // uly
    wide, narrow = kvq.shape[1] // HEAD, feat // HEAD
    at = wide * SLOTS

    with jax.named_scope("rows_in"):
        kvq = pack_rows(me[None], [kvq], place, ctx, TAIL)
        kvq = exchange(add_tail(ahead[0], hop, kvq), "ctx")

    with jax.named_scope("cotangent_in"):
        cot = pack_rows(me[None], cotangent_blocks(cotangent, me, feat), place, ctx)
        cot = exchange(cot, "ctx")

    with jax.named_scope("forward"):
        kvq, more = unpack_rows(kvq, slot_source, wide)
        att, stats = forward_attention(kvq, doc_row)
        inv_root = lax.rsqrt(sum_over(stats[7:8, :], "uly", ULY_ROUNDS) / width + 1e-06)

    with jax.named_scope("normed_out"):
        normed_sent, normed_slots = pack_normed_slots(att, inv_root, gain_row, slot_source, ctx)
        normed = exchange(normed_sent, "ctx")

    with jax.named_scope("backward"):
        cot, cross, gain_part = unpack_cotangent(
            cot, more, slot_source, att, inv_root, gain_row
        )
        cross = sum_over(cross, "uly", ULY_ROUNDS)
        grads = backward_attention(kvq, doc_row, att, cot, stats, inv_root, cross, gain_row)

    with jax.named_scope("grads_out"):
        high = lax.reduce_precision(gain_part, 8, 7)
        part = jnp.concatenate([high, gain_part - high], axis=1).astype(BF16).reshape(-1, HEAD)
        part = jnp.pad(part, ((0, TAIL - part.shape[0]), (0, 0)))
        grads = pack_grads(grads, normed_slots, part, slot_source, ctx)
        grads, normed = lax.optimization_barrier((grads, normed))
        grads = exchange(grads, "ctx")

    with jax.named_scope("normed_rows"):
        normed = all_shifts(return_rows(me[None], normed, place, narrow, uly), "uly")
        grads, *normed = lax.optimization_barrier((grads, *normed))

    with jax.named_scope("passed_back"):
        hop = grads[:, at : at + TAIL, :][back[:, 0]]
        grads, hop = lax.optimization_barrier((grads, hop))
        hop = exchange(hop, "ctx")

    with jax.named_scope("grad_rows"):
        rows_back = all_shifts(return_rows(me[None], grads, place, wide, uly), "uly")

    with jax.named_scope("gain_out"):
        parts = grads[:, at + TAIL : at + TAIL + 2 * narrow, :].astype(F32)
        gain_total = jnp.sum(parts[:, 0:narrow] + parts[:, narrow:], axis=0).reshape(1, feat)

    with jax.named_scope("merge"):
        hop = with_gain(hop.reshape(ctx, TAIL * HEAD), gain_total)
        return merge_rows(me[None], via, all_shifts([hop] * uly, "uly"), rows_back, normed)


def per_device(queries, keys, values, cotangent, norm_gain, owner_of_row, arrival, doc_start):
    tok, width = queries.shape
    uly, ctx = lax.axis_size("uly"), lax.axis_size("ctx")
    rows = tok * uly
    capacity = 2 * rows // ctx
    feat = width // uly
    me, here = lax.axis_index("uly"), lax.axis_index("ctx")

    with jax.named_scope("plan"):
        place, via, position, counts = plan_rows(owner_of_row[None, :], ctx, capacity)
        arrival_row = arrival[None, :]
        doc_row = doc_start[None, :]
        gain_row = lax.dynamic_slice_in_dim(norm_gain, me * feat, feat)[None, :]

    with jax.named_scope("rows_over_uly"):
        kvq = jnp.concatenate([x.reshape(tok, uly, -1) for x in (keys, values, queries)], axis=2)
        kvq = exchange(kvq.transpose(1, 0, 2), "uly").reshape(rows, -1)
        picked = all_shifts(pick_rows(me[None], via, cotangent, uly, ctx), "uly")

    with jax.named_scope("first_hop"):
        hop = exchange(join_picked(counts, via, kvq, picked), "ctx")
        table = hop[:, TAIL, :]
        fits, slot_source, ahead, back = choose(here[None], table, arrival_row, capacity)

    outs = passed_path(
        me, kvq, hop, cotangent, place, via, slot_source, ahead, back, doc_row, gain_row
    )

    def keep(outs, cotangent, kvq):
        return list(outs)

    def padded(outs, cotangent, kvq):
        return list(padded_path(me, kvq, cotangent, position, arrival_row, doc_row, gain_row))

    outs = lax.cond(fits[0, 0] == 1, keep, padded, outs, cotangent, kvq)
    return (*outs[0:4], outs[4].reshape(width))


def solution(mesh):
    split = P(("ctx", "uly"), None)
    plan = P("ctx")
    return jax.shard_map(
        per_device,
        mesh=mesh,
        in_specs=(split, split, split, split, P(), plan, plan, plan),
        out_specs=(split, split, split, split, P()),
        check_vma=False,
    )
```
